256 devices in a mesh: ia: 16 (over y, x), ja: 4 (over z_hi, core), ta: 4 (over z_lo).
Axes of the slice: x: 4, y: 4, z: 8 (z_hi: 2, z_lo: 4; z = z_hi * 4 + z_lo), core: 2. Of those that a mesh axis runs over, the one named last changes fastest.
Arguments:
- readings: bfloat16 [48, 4096, 4096], P('ta', 'ia', 'ja'), may hold values from 0.049804688 to 20
- factor_first: float32 [4096, 128], P(('ia', 'ja', 'ta')), may hold values from 0.1 to 0.4
- factor_second: float32 [128, 4096], P('ia', ('ja', 'ta')), may hold values from 0.1 to 0.4
- factor_time: float32 [48, 128], P('ta'), may hold values from 0.05 to 0.4
- mean_first: float32 [4096, 128], P(('ia', 'ja', 'ta')), may hold values from -4 to 4
- square_first: float32 [4096, 128], P(('ia', 'ja', 'ta')), may hold values from 0.3 to 5
- mean_second: float32 [128, 4096], P('ia', ('ja', 'ta')), may hold values from -4 to 4
- square_second: float32 [128, 4096], P('ia', ('ja', 'ta')), may hold values from 0.3 to 5
- mean_time: float32 [48, 128], P('ta'), may hold values from -4 to 4
- square_time: float32 [48, 128], P('ta'), may hold values from 0.3 to 5
Outputs:
- result_first: float32 [4096, 128], P(('ia', 'ja', 'ta'))
- result_second: float32 [128, 4096], P('ia', ('ja', 'ta'))
- result_time: float32 [48, 128], P('ta')
- drift_first: float32 [4096, 128], P(('ia', 'ja', 'ta'))
- spread_first: float32 [4096, 128], P(('ia', 'ja', 'ta'))
- drift_second: float32 [128, 4096], P('ia', ('ja', 'ta'))
- spread_second: float32 [128, 4096], P('ia', ('ja', 'ta'))
- drift_time: float32 [48, 128], P('ta')
- spread_time: float32 [48, 128], P('ta')
The draws below stay inside these ranges and needn't reach their ends.
All inputs are finite; a program needn't handle non-finite values.
Results may differ from the reference program's by a relative error of at most 0.0024.
Values may be sent and summed in bfloat16 or wider, within the bound.
No kernel may reach another device: no remote copies, remote signals or barrier semaphores. Data moves between devices by JAX's collectives and lax.ppermute only.
A program may use at most 64 MiB of HBM per device.

```python
import math
import jax
import jax.numpy as jnp
from jax import lax

R = 128
STEPS = 2
ADAM_STEP = 20
I = 4096
J = 4096
K = 48


def block_levels(rng, shape, cuts, least, largest):
    factor_of = 1.0
    for dim, blocks in cuts:
        steps = jax.random.uniform(jax.random.fold_in(jax.random.fold_in(rng, 6), dim), (blocks,), jnp.float32, least / len(cuts), largest / len(cuts))
        factor_of = factor_of * jnp.repeat(jnp.exp(steps), shape[dim] // blocks).reshape((-1,) + (1,) * (len(shape) - 1 - dim))
    return factor_of


def normal_values(rng, extent, deviation, bound, shards=(), dtype=jnp.bfloat16):
    entries = jax.random.normal(rng, extent, jnp.float32) * deviation
    if len(shards) > 0:
        entries = block_levels(rng, extent, shards, -0.22, 0.18) * entries
    return jnp.clip(entries, min=-bound, max=bound).astype(dtype)


def setup_inputs(seed: int = 0) -> dict:
    key_list = jax.random.split(jax.random.key(seed), 11)
    readings = jnp.clip(jnp.exp(math.log(20.0) - 5.9953784 * jax.random.uniform(key_list[0], (K, I, J), jnp.float32) ** block_levels(key_list[0], (K, I, J), ((0, 4), (1, 16), (2, 4)), -0.2, 0.2)), 0.049804688, 20.0).astype(jnp.bfloat16)
    factor_first = jnp.clip(jnp.exp(math.log(0.4) - 1.3862944 * jax.random.uniform(key_list[1], (I, R), jnp.float32) ** block_levels(key_list[1], (I, R), ((0, 256),), -0.2, 0.2)), 0.1, 0.4)
    factor_second = jnp.clip(jnp.exp(math.log(0.4) - 1.3862944 * jax.random.uniform(key_list[2], (R, J), jnp.float32) ** block_levels(key_list[2], (R, J), ((0, 16), (1, 16)), -0.2, 0.2)), 0.1, 0.4)
    factor_time = jnp.clip(jnp.exp(math.log(0.4) - 2.0794415 * jax.random.uniform(key_list[3], (K, R), jnp.float32) ** block_levels(key_list[3], (K, R), ((0, 4),), -0.2, 0.2)), 0.05, 0.4)
    mean_first = normal_values(key_list[4], (I, R), 1.0, 4.0, ((0, 256),), jnp.float32)
    square_first = jnp.clip(jnp.exp(math.log(5.0) - 2.8134107 * jax.random.uniform(key_list[5], (I, R), jnp.float32) ** block_levels(key_list[5], (I, R), ((0, 256),), -0.2, 0.2)), 0.3, 5.0)
    mean_second = normal_values(key_list[6], (R, J), 1.0, 4.0, ((0, 16), (1, 16)), jnp.float32)
    square_second = jnp.clip(jnp.exp(math.log(5.0) - 2.8134107 * jax.random.uniform(key_list[7], (R, J), jnp.float32) ** block_levels(key_list[7], (R, J), ((0, 16), (1, 16)), -0.2, 0.2)), 0.3, 5.0)
    mean_time = normal_values(key_list[8], (K, R), 1.0, 4.0, ((0, 4),), jnp.float32)
    square_time = jnp.clip(jnp.exp(math.log(5.0) - 2.8134107 * jax.random.uniform(key_list[9], (K, R), jnp.float32) ** block_levels(key_list[9], (K, R), ((0, 4),), -0.2, 0.2)), 0.3, 5.0)
    return dict(readings=readings, factor_first=factor_first, factor_second=factor_second, factor_time=factor_time, mean_first=mean_first, square_first=square_first, mean_second=mean_second, square_second=square_second, mean_time=mean_time, square_time=square_time)


beta_one = 0.9
beta_two = 0.99
step_rate = 0.02
tiny_eps = 1e-08

def gradients(readings, a16, b16, c16):
    af = a16.astype(jnp.float32)
    cf = c16.astype(jnp.float32)

    def per_time(carry, inputs):
        acc_first, acc_second = carry
        slab, c_row = inputs
        scaled = (af * c_row[None, :]).astype(jnp.bfloat16)
        model = jnp.dot(scaled, b16, preferred_element_type=jnp.float32)
        slope = (1.0 / model - slab.astype(jnp.float32) / (model * model)).astype(jnp.bfloat16)
        cross = jnp.dot(slope, b16.T, preferred_element_type=jnp.float32)
        acc_first = acc_first + cross * c_row[None, :]
        acc_second = acc_second + jnp.dot(scaled.T, slope, preferred_element_type=jnp.float32)
        time_row = lax.optimization_barrier(jnp.sum(cross * af, axis=0))
        return ((acc_first, acc_second), time_row)
    start = (jnp.zeros((I, R), jnp.float32), jnp.zeros((R, J), jnp.float32))
    (acc_first, acc_second), acc_time = lax.scan(per_time, start, (readings, cf))
    return (acc_first * (R / (J * K)), acc_second * (R / (I * K)), acc_time * (R / (I * J)))

def adam(value, grad, mean, square, count):
    drift = beta_one * mean + (1.0 - beta_one) * grad
    spread = beta_two * square + (1.0 - beta_two) * grad * grad
    fixed_one = 1.0 - beta_one ** count
    fixed_two = 1.0 - beta_two ** count
    value = value - step_rate * (drift / fixed_one) / (jnp.sqrt(spread / fixed_two) + tiny_eps)
    return (value, drift, spread)

def reference(readings, factor_first, factor_second, factor_time, mean_first, square_first, mean_second, square_second, mean_time, square_time):
    for step in range(STEPS):
        count = ADAM_STEP + step + 1
        grad_first, grad_second, grad_time = gradients(readings, factor_first.astype(jnp.bfloat16), factor_second.astype(jnp.bfloat16), factor_time.astype(jnp.bfloat16))
        factor_first, mean_first, square_first = adam(factor_first, grad_first, mean_first, square_first, count)
        factor_second, mean_second, square_second = adam(factor_second, grad_second, mean_second, square_second, count)
        factor_time, mean_time, square_time = adam(factor_time, grad_time, mean_time, square_time, count)
    return (factor_first, factor_second, factor_time, mean_first, square_first, mean_second, square_second, mean_time, square_time)
```

```python
import jax
import jax.numpy as jnp
from jax import lax
from jax.sharding import PartitionSpec as P

STEPS = 2
ADAM_STEP = 20


beta_one = 0.9
beta_two = 0.99
step_rate = 0.02
tiny_eps = 1e-08


def adam(value, grad, mean, square, count):
    drift = beta_one * mean + (1.0 - beta_one) * grad
    spread = beta_two * square + (1.0 - beta_two) * grad * grad
    fixed_one = 1.0 - beta_one**count
    fixed_two = 1.0 - beta_two**count
    value = value - step_rate * (drift / fixed_one) / (jnp.sqrt(spread / fixed_two) + tiny_eps)
    return (value, drift, spread)


def gather_factors(factor_first, factor_second, ni, nj, nt):
    rows, rank = factor_first.shape
    ranks, cols = factor_second.shape
    ja = lax.axis_index("ja")
    a_piece = factor_first.astype(jnp.bfloat16)
    b_piece = factor_second.astype(jnp.bfloat16)
    b_flat = jnp.concatenate([b_piece[:, :rank], b_piece[:, rank:]], axis=0)
    both = jnp.concatenate([a_piece, b_flat], axis=0)
    got = lax.all_to_all(
        jnp.broadcast_to(both, (nj * nt,) + both.shape), ("ja", "ta"), 0, 0
    )
    a16 = got[:, :rows].reshape(nj * nt * rows, rank)
    mine = lax.dynamic_slice_in_dim(got[:, rows:], ja * nt, nt, axis=0)
    halves = []
    for t in range(nt):
        halves += [mine[t, :ranks], mine[t, ranks:]]
    flat = jnp.concatenate(
        [jnp.concatenate(halves[:nt], axis=1), jnp.concatenate(halves[nt:], axis=1)], axis=0
    )
    got = lax.all_to_all(jnp.broadcast_to(flat, (ni,) + flat.shape), "ia", 0, 0)
    width = flat.shape[1]
    b16 = jnp.concatenate(
        [got[:, :ranks].reshape(ni * ranks, width), got[:, ranks:].reshape(ni * ranks, width)],
        axis=1,
    )
    return a16, b16


def reduce_parts(part_first, part_second, part_time, ni, nj, nt):
    rank = part_first.shape[1]
    ja, ta = lax.axis_index("ja"), lax.axis_index("ta")
    n_time = part_time.shape[0]
    ranks = part_second.shape[0] // ni
    cols = part_second.shape[1]
    time_pad = jnp.pad(part_time, ((0, 2 * ranks - n_time), (0, 0)))
    time_flat = jnp.concatenate([time_pad[:ranks], time_pad[ranks:]], axis=1)
    slots = jnp.concatenate(
        [
            part_second.reshape(ni, ranks, cols),
            jnp.broadcast_to(time_flat, (ni,) + time_flat.shape),
        ],
        axis=2,
    )
    got = jnp.sum(lax.all_to_all(slots, "ia", 0, 0), axis=0)
    time_flat = got[:, cols:]
    time_rows = jnp.concatenate([time_flat[:, :rank], time_flat[:, rank:]], axis=0)
    wide = cols // nt
    second = jnp.stack(
        [
            jnp.concatenate(
                [got[:, t * wide : t * wide + rank], got[:, t * wide + rank : (t + 1) * wide]],
                axis=0,
            )
            for t in range(nt)
        ]
    )
    same = jnp.arange(nj) == ja
    extra = jnp.where(
        same[:, None, None, None], second[None], time_rows[None, None]
    ).reshape(nj * nt, 2 * ranks, rank)
    rows = part_first.shape[0] // (nj * nt)
    slots = jnp.concatenate([part_first.reshape(nj * nt, rows, rank), extra], axis=1)
    got = lax.all_to_all(slots, ("ja", "ta"), 0, 0)
    grad_first = jnp.sum(got[:, :rows], axis=0)
    extra = got[:, rows:]
    mine = jnp.sum(lax.dynamic_slice_in_dim(extra, ja * nt, nt, axis=0), axis=0)
    grad_second = jnp.concatenate([mine[:ranks], mine[ranks:]], axis=1)
    others = lax.dynamic_index_in_dim(
        extra.reshape(nj, nt, 2 * ranks, rank), ta, axis=1, keepdims=False
    )
    grad_time = jnp.sum(jnp.where(same[:, None, None], time_rows[None], others), axis=0)
    return grad_first, grad_second, grad_time[:n_time]


def body(
    readings,
    factor_first,
    factor_second,
    factor_time,
    mean_first,
    square_first,
    mean_second,
    square_second,
    mean_time,
    square_time,
):
    ni, nj, nt = lax.axis_size("ia"), lax.axis_size("ja"), lax.axis_size("ta")
    whole_i = readings.shape[1] * ni
    whole_j = readings.shape[2] * nj
    whole_k = readings.shape[0] * nt
    rank = factor_first.shape[1]
    for step in range(STEPS):
        count = ADAM_STEP + step + 1
        a16, b16 = gather_factors(factor_first, factor_second, ni, nj, nt)
        c16 = factor_time.astype(jnp.bfloat16)
        af = a16.astype(jnp.float32)
        cf = c16.astype(jnp.float32)
        scaled = (af[None, :, :] * cf[:, None, :]).astype(jnp.bfloat16)
        model = lax.dot_general(
            scaled, b16, (((2,), (0,)), ((), ())), preferred_element_type=jnp.float32
        )
        slope = (1.0 / model - readings.astype(jnp.float32) / (model * model)).astype(jnp.bfloat16)
        cross = lax.dot_general(
            slope, b16, (((2,), (1,)), ((), ())), preferred_element_type=jnp.float32
        )
        part_second = lax.dot_general(
            scaled, slope, (((0, 1), (0, 1)), ((), ())), preferred_element_type=jnp.float32
        )
        part_first = jnp.sum(cross * cf[:, None, :], axis=0)
        part_time = jnp.sum(cross * af[None, :, :], axis=1)
        grad_first, grad_second, grad_time = reduce_parts(
            part_first, part_second, part_time, ni, nj, nt
        )
        grad_first = grad_first * (rank / (whole_j * whole_k))
        grad_second = grad_second * (rank / (whole_i * whole_k))
        grad_time = grad_time * (rank / (whole_i * whole_j))
        factor_first, mean_first, square_first = adam(
            factor_first, grad_first, mean_first, square_first, count
        )
        factor_second, mean_second, square_second = adam(
            factor_second, grad_second, mean_second, square_second, count
        )
        factor_time, mean_time, square_time = adam(
            factor_time, grad_time, mean_time, square_time, count
        )
    return (
        factor_first,
        factor_second,
        factor_time,
        mean_first,
        square_first,
        mean_second,
        square_second,
        mean_time,
        square_time,
    )


def solution(mesh):
    first = P(("ia", "ja", "ta"), None)
    second = P("ia", ("ja", "ta"))
    time = P("ta", None)
    return jax.shard_map(
        body,
        mesh=mesh,
        in_specs=(
            P("ta", "ia", "ja"),
            first,
            second,
            time,
            first,
            first,
            second,
            second,
            time,
            time,
        ),
        out_specs=(first, second, time, first, first, second, second, time, time),
        check_vma=False,
    )
```

```python
import jax
import jax.numpy as jnp
from jax import lax
from jax.sharding import PartitionSpec as P

STEPS = 2
ADAM_STEP = 20


beta_one = 0.9
beta_two = 0.99
step_rate = 0.02
tiny_eps = 1e-08


def adam(value, grad, mean, square, count):
    drift = beta_one * mean + (1.0 - beta_one) * grad
    spread = beta_two * square + (1.0 - beta_two) * grad * grad
    fixed_one = 1.0 - beta_one**count
    fixed_two = 1.0 - beta_two**count
    value = value - step_rate * (drift / fixed_one) / (jnp.sqrt(spread / fixed_two) + tiny_eps)
    return (value, drift, spread)


def swap(x, axis, k):
    n = lax.axis_size(axis)
    return lax.ppermute(x, axis, [(i, i ^ k) for i in range(n)])


def pick(flag, x, y):
    return jnp.where(flag, y, x), jnp.where(flag, x, y)


def gather_ta(x):
    ta = lax.axis_index("ta")
    p = [x] + [swap(x, "ta", k) for k in (1, 2, 3)]
    odd, high = (ta & 1) == 1, (ta & 2) == 2
    q0, q1 = pick(odd, p[0], p[1])
    q2, q3 = pick(odd, p[2], p[3])
    q0, q2 = pick(high, q0, q2)
    q1, q3 = pick(high, q1, q3)
    return [q0, q1, q2, q3]


def sum_ta(pieces):
    ta = lax.axis_index("ta")
    got = [pieces(ta)] + [swap(pieces(ta ^ k), "ta", k) for k in (1, 2, 3)]
    return (got[0] + got[1]) + (got[2] + got[3])


def gather_first(piece):
    ja = lax.axis_index("ja")
    x = jnp.concatenate(gather_ta(piece), axis=0)
    for k in (1, 2):
        low, high = pick((ja & k) == k, x, swap(x, "ja", k))
        x = jnp.concatenate([low, high], axis=0)
    return x


def reduce_first(part, part_time):
    ja = lax.axis_index("ja")
    n_time = part_time.shape[0]
    pad = 16 - n_time
    part_time = jnp.pad(part_time, ((0, pad), (0, 0)))
    for k in (1, 2):
        half = part.shape[0] // 2
        high = (ja & k) == k
        if k == 1:
            quarter = half // 2
            q = [part[n * quarter : (n + 1) * quarter] for n in range(4)]
            keep0, send0 = pick(high, q[0], q[1])
            keep1, send1 = pick(high, q[2], q[3])
            keep = jnp.concatenate([keep0, keep1], axis=0)
            send = jnp.concatenate([send0, send1, part_time], axis=0)
        else:
            keep, send = pick(high, part[:half], part[half:])
            send = jnp.concatenate([send, part_time], axis=0)
        got = swap(send, "ja", k)
        part = keep + got[:half]
        part_time = part_time + got[half:]
    rows = part.shape[0] // 4
    mine = sum_ta(lambda t: lax.dynamic_slice_in_dim(part, t * rows, rows, axis=0))
    return mine, part_time


def flatten(piece):
    half = piece.shape[1] // 2
    return jnp.concatenate([piece[:, :half], piece[:, half:]], axis=0)


def spread_second(wide, time_parts):
    ni = lax.axis_size("ia")
    ranks, cols = wide.shape
    half = cols // 2
    flat = jnp.concatenate([wide[:, :half], wide[:, half:]], axis=0)
    if time_parts is not None:
        rows, rank = time_parts.shape
        t_rows = rows * rank // half
        per = half // rank
        line = jnp.concatenate([time_parts[n * t_rows : (n + 1) * t_rows] for n in range(per)], axis=1)
        top = lax.reduce_precision(line, 8, 7)
        low = (line - top).astype(jnp.bfloat16)
        flat = jnp.concatenate([flat, top.astype(jnp.bfloat16), low], axis=0)
    got = lax.all_to_all(jnp.broadcast_to(flat, (ni,) + flat.shape), "ia", 0, 0)
    b16 = jnp.concatenate(
        [
            got[:, :ranks].reshape(ni * ranks, half),
            got[:, ranks : 2 * ranks].reshape(ni * ranks, half),
        ],
        axis=1,
    )
    if time_parts is None:
        return b16, None
    top = got[:, 2 * ranks : 2 * ranks + t_rows].astype(jnp.float32)
    low = got[:, 2 * ranks + t_rows :].astype(jnp.float32)
    line = jnp.sum(top + low, axis=0)
    time_sum = jnp.concatenate([line[:, n * rank : (n + 1) * rank] for n in range(per)], axis=0)
    return b16, time_sum


def parts(readings, a16, b16, c16):
    af = a16.astype(jnp.float32)
    cf = c16.astype(jnp.float32)
    scaled = (af[None, :, :] * cf[:, None, :]).astype(jnp.bfloat16)
    model = lax.dot_general(
        scaled, b16, (((2,), (0,)), ((), ())), preferred_element_type=jnp.float32
    )
    slope = (1.0 / model - readings.astype(jnp.float32) / (model * model)).astype(jnp.bfloat16)
    part_second = lax.dot_general(
        scaled, slope, (((0, 1), (0, 1)), ((), ())), preferred_element_type=jnp.float32
    )
    cross = lax.dot_general(
        slope, b16, (((2,), (1,)), ((), ())), preferred_element_type=jnp.float32
    )
    part_first = jnp.sum(cross * cf[:, None, :], axis=0)
    part_time = jnp.sum(cross * af[None, :, :], axis=1)
    return part_first, part_second, part_time


def body(
    readings,
    factor_first,
    factor_second,
    factor_time,
    mean_first,
    square_first,
    mean_second,
    square_second,
    mean_time,
    square_time,
):
    ni, nj, nt = lax.axis_size("ia"), lax.axis_size("ja"), lax.axis_size("ta")
    whole_i = readings.shape[1] * ni
    whole_j = readings.shape[2] * nj
    whole_k = readings.shape[0] * nt
    n_time, rank = factor_time.shape
    scale_first = rank / (whole_j * whole_k)
    scale_second = rank / (whole_i * whole_k)
    scale_time = rank / (whole_i * whole_j)
    ranks, cols = factor_second.shape
    ta = lax.axis_index("ta")

    pieces = gather_ta(flatten(factor_second.astype(jnp.bfloat16)))
    wide = jnp.concatenate([p for q in pieces for p in (q[:ranks], q[ranks:])], axis=1)
    a16 = gather_first(factor_first.astype(jnp.bfloat16))
    b16, _ = spread_second(wide, None)
    c16 = factor_time.astype(jnp.bfloat16)
    part_first, part_second, part_time = parts(readings, a16, b16, c16)

    state = jnp.concatenate([factor_second, mean_second, square_second], axis=0)
    state, part_second = lax.optimization_barrier((state, part_second))
    state = jnp.concatenate(gather_ta(state), axis=1)

    mine_first, time_ja = reduce_first(part_first, part_time)
    got = lax.all_to_all(part_second.reshape(ni, ranks, nt * cols), "ia", 0, 0)
    second = jnp.sum(got, axis=0)
    second = (second + swap(second, "ta", 1)) + (swap(second, "ta", 2) + swap(second, "ta", 3))
    count = ADAM_STEP + 1
    wide_second, wide_mean, wide_square = adam(
        state[:ranks],
        second * scale_second,
        state[ranks : 2 * ranks],
        state[2 * ranks :],
        count,
    )
    factor_first, mean_first, square_first = adam(
        factor_first, mine_first * scale_first, mean_first, square_first, count
    )

    a16 = gather_first(factor_first.astype(jnp.bfloat16))
    b16, time_sum = spread_second(wide_second.astype(jnp.bfloat16), time_ja)
    factor_time, mean_time, square_time = adam(
        factor_time, time_sum[:n_time] * scale_time, mean_time, square_time, count
    )
    c16 = factor_time.astype(jnp.bfloat16)
    part_first, part_second, part_time = parts(readings, a16, b16, c16)
    mine_first, time_ja = reduce_first(part_first, part_time)
    got = lax.all_to_all(part_second.reshape(ni, ranks, nt * cols), "ia", 0, 0)
    second = jnp.sum(got, axis=0)
    mine_second = sum_ta(lambda t: lax.dynamic_slice_in_dim(second, t * cols, cols, axis=1))
    time_sum = jnp.sum(
        lax.all_to_all(jnp.broadcast_to(time_ja, (ni,) + time_ja.shape), "ia", 0, 0), axis=0
    )
    count = ADAM_STEP + 2
    own = lambda x: lax.dynamic_slice_in_dim(x, ta * cols, cols, axis=1)
    factor_first, mean_first, square_first = adam(
        factor_first, mine_first * scale_first, mean_first, square_first, count
    )
    factor_second, mean_second, square_second = adam(
        own(wide_second), mine_second * scale_second, own(wide_mean), own(wide_square), count
    )
    factor_time, mean_time, square_time = adam(
        factor_time, time_sum[:n_time] * scale_time, mean_time, square_time, count
    )
    return (
        factor_first,
        factor_second,
        factor_time,
        mean_first,
        square_first,
        mean_second,
        square_second,
        mean_time,
        square_time,
    )


def solution(mesh):
    first = P(("ia", "ja", "ta"), None)
    second = P("ia", ("ja", "ta"))
    time = P("ta", None)
    return jax.shard_map(
        body,
        mesh=mesh,
        in_specs=(
            P("ta", "ia", "ja"),
            first,
            second,
            time,
            first,
            first,
            second,
            second,
            time,
            time,
        ),
        out_specs=(first, second, time, first, first, second, second, time, time),
        check_vma=False,
    )
```

```python
import jax
import jax.numpy as jnp
from jax import lax
from jax.sharding import PartitionSpec as P

STEPS = 2
ADAM_STEP = 20


beta_one = 0.9
beta_two = 0.99
step_rate = 0.02
tiny_eps = 1e-08


def adam(value, grad, mean, square, count):
    drift = beta_one * mean + (1.0 - beta_one) * grad
    spread = beta_two * square + (1.0 - beta_two) * grad * grad
    fixed_one = 1.0 - beta_one**count
    fixed_two = 1.0 - beta_two**count
    value = value - step_rate * (drift / fixed_one) / (jnp.sqrt(spread / fixed_two) + tiny_eps)
    return (value, drift, spread)


def swap(x, axis, k):
    n = lax.axis_size(axis)
    return lax.ppermute(x, axis, [(i, i ^ k) for i in range(n)])


def pick(flag, x, y):
    return jnp.where(flag, y, x), jnp.where(flag, x, y)


def exchange_ta(slots):
    return lax.all_to_all(slots, "ta", 0, 0)


def stack_columns(x):
    return jnp.concatenate([x[:, n * 128 : (n + 1) * 128] for n in range(x.shape[1] // 128)], axis=0)


def unstack_columns(x, ranks):
    return jnp.concatenate([x[n * ranks : (n + 1) * ranks] for n in range(x.shape[0] // ranks)], axis=1)


def gather_ja(x):
    ja = lax.axis_index("ja")
    for k in (1, 2):
        low, high = pick((ja & k) == k, x, swap(x, "ja", k))
        x = jnp.concatenate([low, high], axis=0)
    return x


def gather_pairs(piece):
    ja, ta = lax.axis_index("ja"), lax.axis_index("ta")
    x = piece[None]
    for k in (2, 1):
        low, high = pick((ja & k) == k, x, swap(x, "ja", k))
        x = jnp.concatenate([low, high], axis=0) if k == 2 else jnp.stack([low, high], axis=1)
    x = x.reshape((-1,) + piece.shape)
    p = [x] + [swap(x, "ta", k) for k in (1, 2, 3)]
    odd, high = (ta & 1) == 1, (ta & 2) == 2
    q0, q1 = pick(odd, p[0], p[1])
    q2, q3 = pick(odd, p[2], p[3])
    q0, q2 = pick(high, q0, q2)
    q1, q3 = pick(high, q1, q3)
    return jnp.stack([q0, q1, q2, q3], axis=1).reshape(-1, piece.shape[1])


def reduce_ja(part, part_time):
    ja = lax.axis_index("ja")
    for k in (1, 2):
        half = part.shape[0] // 2
        high = (ja & k) == k
        if k == 1:
            quarter = half // 2
            q = [part[n * quarter : (n + 1) * quarter] for n in range(4)]
            keep0, send0 = pick(high, q[0], q[1])
            keep1, send1 = pick(high, q[2], q[3])
            keep = jnp.concatenate([keep0, keep1], axis=0)
            send = [send0, send1]
        else:
            keep, send = pick(high, part[:half], part[half:])
            send = [send]
        if part_time is not None:
            send = send + [part_time]
        got = swap(jnp.concatenate(send, axis=0), "ja", k)
        part = keep + got[:half]
        if part_time is not None:
            part_time = part_time + got[half:]
    return part, part_time


def sum_ja(x):
    for k in (1, 2):
        x = x + swap(x, "ja", k)
    return x


def spread_second(wide, time_parts):
    ni = lax.axis_size("ia")
    ranks, cols = wide.shape
    half = cols // 2
    flat = jnp.concatenate([wide[:, :half], wide[:, half:]], axis=0)
    if time_parts is not None:
        rows, rank = time_parts.shape
        t_rows = rows * rank // half
        per = half // rank
        line = jnp.concatenate([time_parts[n * t_rows : (n + 1) * t_rows] for n in range(per)], axis=1)
        top = lax.reduce_precision(line, 8, 7)
        low = (line - top).astype(jnp.bfloat16)
        flat = jnp.concatenate([flat, top.astype(jnp.bfloat16), low], axis=0)
    got = lax.all_to_all(jnp.broadcast_to(flat, (ni,) + flat.shape), "ia", 0, 0)
    b16 = jnp.concatenate(
        [
            got[:, :ranks].reshape(ni * ranks, half),
            got[:, ranks : 2 * ranks].reshape(ni * ranks, half),
        ],
        axis=1,
    )
    if time_parts is None:
        return b16, None
    top = got[:, 2 * ranks : 2 * ranks + t_rows].astype(jnp.float32)
    low = got[:, 2 * ranks + t_rows :].astype(jnp.float32)
    line = jnp.sum(top + low, axis=0)
    time_sum = jnp.concatenate([line[:, n * rank : (n + 1) * rank] for n in range(per)], axis=0)
    return b16, time_sum


def parts(readings, a16, b16, c16):
    af = a16.astype(jnp.float32)
    cf = c16.astype(jnp.float32)
    scaled = (af[None, :, :] * cf[:, None, :]).astype(jnp.bfloat16)
    model = lax.dot_general(
        scaled, b16, (((2,), (0,)), ((), ())), preferred_element_type=jnp.float32
    )
    slope = (1.0 / model - readings.astype(jnp.float32) / (model * model)).astype(jnp.bfloat16)
    part_second = lax.dot_general(
        scaled, slope, (((0, 1), (0, 1)), ((), ())), preferred_element_type=jnp.float32
    )
    slope, part_second = lax.optimization_barrier((slope, part_second))
    cross = lax.dot_general(
        slope, b16, (((2,), (1,)), ((), ())), preferred_element_type=jnp.float32
    )
    part_first = jnp.sum(cross * cf[:, None, :], axis=0)
    part_time = jnp.sum(cross * af[None, :, :], axis=1)
    return part_first, part_second, part_time


def body(
    readings,
    factor_first,
    factor_second,
    factor_time,
    mean_first,
    square_first,
    mean_second,
    square_second,
    mean_time,
    square_time,
):
    ni, nj, nt = lax.axis_size("ia"), lax.axis_size("ja"), lax.axis_size("ta")
    whole_i = readings.shape[1] * ni
    whole_j = readings.shape[2] * nj
    whole_k = readings.shape[0] * nt
    n_time, rank = factor_time.shape
    scale_first = rank / (whole_j * whole_k)
    scale_second = rank / (whole_i * whole_k)
    scale_time = rank / (whole_i * whole_j)
    ranks, cols = factor_second.shape
    ta = lax.axis_index("ta")

    rows = factor_first.shape[0]
    flat = 2 * ranks
    pad_time = ((0, 16 - n_time), (0, 0))

    slot = jnp.concatenate(
        [factor_first]
        + [stack_columns(x) for x in (factor_second, mean_second, square_second)],
        axis=0,
    )
    got = exchange_ta(jnp.broadcast_to(slot, (nt,) + slot.shape))
    a16 = gather_ja(got[:, :rows].astype(jnp.bfloat16).reshape(nt * rows, rank))
    wide_second, wide_mean, wide_square = [
        unstack_columns(got[:, n : n + flat].reshape(nt * flat, rank), ranks)
        for n in (rows, rows + flat, rows + 2 * flat)
    ]
    b16, _ = spread_second(wide_second.astype(jnp.bfloat16), None)
    c16 = factor_time.astype(jnp.bfloat16)
    part_first, part_second, part_time = parts(readings, a16, b16, c16)

    second = jnp.sum(
        lax.all_to_all(part_second.reshape(ni, ranks, nt * cols), "ia", 0, 0), axis=0
    )
    part_first, time_ja = reduce_ja(part_first, jnp.pad(part_time, pad_time))
    second = stack_columns(second)
    slots = jnp.concatenate(
        [part_first.reshape(nt, rows, rank), jnp.broadcast_to(second, (nt,) + second.shape)],
        axis=1,
    )
    got = jnp.sum(exchange_ta(slots), axis=0)
    count = ADAM_STEP + 1
    factor_first, mean_first, square_first = adam(
        factor_first, got[:rows] * scale_first, mean_first, square_first, count
    )
    wide_second, wide_mean, wide_square = adam(
        wide_second, unstack_columns(got[rows:], ranks) * scale_second, wide_mean, wide_square, count
    )

    a16 = gather_pairs(factor_first.astype(jnp.bfloat16))
    b16, time_sum = spread_second(wide_second.astype(jnp.bfloat16), time_ja)
    factor_time, mean_time, square_time = adam(
        factor_time, time_sum[:n_time] * scale_time, mean_time, square_time, count
    )
    c16 = factor_time.astype(jnp.bfloat16)
    part_first, part_second, part_time = parts(readings, a16, b16, c16)
    line = jnp.pad(part_time, pad_time)
    line = jnp.concatenate([line[:ranks], line[ranks:]], axis=1)
    got = jnp.sum(
        lax.all_to_all(
            jnp.concatenate(
                [
                    part_second.reshape(ni, ranks, nt * cols),
                    jnp.broadcast_to(line, (ni,) + line.shape),
                ],
                axis=2,
            ),
            "ia",
            0,
            0,
        ),
        axis=0,
    )
    part_first, _ = reduce_ja(part_first, None)
    line = got[:, nt * cols :]
    time_sum = sum_ja(jnp.concatenate([line[:, :rank], line[:, rank:]], axis=0))
    second = stack_columns(got[:, : nt * cols])
    slots = jnp.concatenate(
        [part_first.reshape(nt, rows, rank), second.reshape(nt, flat, rank)], axis=1
    )
    got = jnp.sum(exchange_ta(slots), axis=0)
    count = ADAM_STEP + 2
    own = lambda x: lax.dynamic_slice_in_dim(x, ta * cols, cols, axis=1)
    factor_first, mean_first, square_first = adam(
        factor_first, got[:rows] * scale_first, mean_first, square_first, count
    )
    factor_second, mean_second, square_second = adam(
        own(wide_second),
        unstack_columns(got[rows:], ranks) * scale_second,
        own(wide_mean),
        own(wide_square),
        count,
    )
    factor_time, mean_time, square_time = adam(
        factor_time, time_sum[:n_time] * scale_time, mean_time, square_time, count
    )
    return (
        factor_first,
        factor_second,
        factor_time,
        mean_first,
        square_first,
        mean_second,
        square_second,
        mean_time,
        square_time,
    )


def solution(mesh):
    first = P(("ia", "ja", "ta"), None)
    second = P("ia", ("ja", "ta"))
    time = P("ta", None)
    return jax.shard_map(
        body,
        mesh=mesh,
        in_specs=(
            P("ta", "ia", "ja"),
            first,
            second,
            time,
            first,
            first,
            second,
            second,
            time,
            time,
        ),
        out_specs=(first, second, time, first, first, second, second, time, time),
        check_vma=False,
    )
```

```python
import jax
import jax.numpy as jnp
from jax import lax
from jax.experimental import pallas as pl
from jax.experimental.pallas import tpu as pltpu
from jax.sharding import PartitionSpec as P

ADAM_STEP = 20


beta_one = 0.9
beta_two = 0.99
step_rate = 0.02
tiny_eps = 1e-08


def adam(value, grad, mean, square, count):
    drift = beta_one * mean + (1.0 - beta_one) * grad
    spread = beta_two * square + (1.0 - beta_two) * grad * grad
    fixed_one = 1.0 - beta_one**count
    fixed_two = 1.0 - beta_two**count
    value = value - step_rate * (drift / fixed_one) / (jnp.sqrt(spread / fixed_two) + tiny_eps)
    return (value, drift, spread)


def swap(x, axis, k):
    n = lax.axis_size(axis)
    return lax.ppermute(x, axis, [(i, i ^ k) for i in range(n)])


def pick(flag, x, y):
    return jnp.where(flag, y, x), jnp.where(flag, x, y)


def gather_ta(x):
    ta = lax.axis_index("ta")
    p = [x] + [swap(x, "ta", k) for k in (1, 2, 3)]
    odd, high = (ta & 1) == 1, (ta & 2) == 2
    q0, q1 = pick(odd, p[0], p[1])
    q2, q3 = pick(odd, p[2], p[3])
    q0, q2 = pick(high, q0, q2)
    q1, q3 = pick(high, q1, q3)
    return [q0, q1, q2, q3]


def stack_columns(x):
    return jnp.concatenate([x[:, n * 128 : (n + 1) * 128] for n in range(x.shape[1] // 128)], axis=0)


def unstack_columns(x, ranks):
    return jnp.concatenate([x[n * ranks : (n + 1) * ranks] for n in range(x.shape[0] // ranks)], axis=1)


def pack_kernel(f0, f1, f2, s0, s1, s2, out, state):
    rows = f0.shape[0]
    ranks = s0.shape[0]
    for p in range(out.shape[0]):
        for n, x in enumerate((s0, s1, s2)):
            for h in (0, 1):
                at = (2 * n + h) * ranks
                out[p, at : at + ranks, :] = x[:, h * 128 : (h + 1) * 128]
        out[p, 6 * ranks :, :] = f0[...]
    for n, x in enumerate((f0, f1, f2)):
        state[n * rows : (n + 1) * rows, :] = x[...]


def pack(copies, firsts, seconds):
    rows, rank = firsts[0].shape
    slots = (copies, rows + 6 * seconds[0].shape[0], rank)
    return pl.pallas_call(
        pack_kernel,
        out_shape=[
            jax.ShapeDtypeStruct(slots, jnp.float32),
            jax.ShapeDtypeStruct((3 * rows, rank), jnp.float32),
        ],
        in_specs=[pl.BlockSpec(memory_space=pltpu.VMEM)] * 6,
        out_specs=[pl.BlockSpec(memory_space=pltpu.VMEM)] * 2,
    )(*firsts, *seconds)


def join_cores(x):
    low, high = pick(lax.axis_index("co") == 1, x, swap(x, "co", 1))
    return jnp.stack([low, high], axis=1)


def gather_first(pair):
    rank = pair.shape[1]
    x = join_cores(pair.reshape(2, -1, rank))
    x = x.reshape((-1,) + x.shape[2:])
    return jnp.stack(gather_ta(x), axis=1).reshape(-1, rank)


def core_half(part, extra):
    one = lax.axis_index("co") == 1
    quarter = part.shape[0] // 4
    q = [part[n * quarter : (n + 1) * quarter] for n in range(4)]
    keep0, send0 = pick(one, q[0], q[1])
    keep1, send1 = pick(one, q[2], q[3])
    keep = jnp.concatenate([keep0, keep1], axis=0)
    got = swap(jnp.concatenate([send0, send1] + extra, axis=0), "co", 1)
    half = keep.shape[0]
    return keep + got[:half], [extra[0] + got[half:]] if extra else []


def bf16_pair(x):
    top = lax.reduce_precision(x, 8, 7)
    return [top.astype(jnp.bfloat16), (x - top).astype(jnp.bfloat16)]


def fold(x, rows):
    return jnp.concatenate([x[n * rows : (n + 1) * rows] for n in range(x.shape[0] // rows)], axis=1)


def time_of(got, rank):
    r = got.shape[1] // 2
    line = jnp.sum(got[:, :r].astype(jnp.float32) + got[:, r:].astype(jnp.float32), axis=0)
    return jnp.concatenate(
        [line[:, n * rank : (n + 1) * rank] for n in range(line.shape[1] // rank)], axis=0
    )


def spread_slots(stacked, extra):
    ni = lax.axis_size("ia")
    wide = stacked.astype(jnp.bfloat16)
    half = wide.shape[0] // 2
    ranks = half // 4
    flat = jnp.concatenate(
        [unstack_columns(wide[:half], ranks), unstack_columns(wide[half:], ranks)] + extra, axis=0
    )
    return jnp.broadcast_to(flat, (ni,) + flat.shape)


def spread_second(slots, ranks):
    ni, _, width = slots.shape
    got = lax.all_to_all(slots, "ia", 0, 0)
    b16 = jnp.concatenate(
        [
            got[:, :ranks].reshape(ni * ranks, width),
            got[:, ranks : 2 * ranks].reshape(ni * ranks, width),
        ],
        axis=1,
    )
    return b16, got[:, 2 * ranks :]


def second_slots(part, ni, extra):
    ranks = part.shape[0] // ni
    half = part.shape[1] // 2
    cut = part.astype(jnp.bfloat16).reshape(ni, ranks, 2, half)
    slots = [cut[:, :, 0], cut[:, :, 1]]
    slots += [jnp.broadcast_to(x, (ni,) + x.shape) for x in extra]
    return jnp.concatenate(slots, axis=1)


def sum_second(slots, ranks):
    got = lax.all_to_all(slots, "ia", 0, 0)
    total = jnp.sum(got[:, : 2 * ranks].astype(jnp.float32), axis=0)
    return jnp.concatenate([total[:ranks], total[ranks:]], axis=1), got[:, 2 * ranks :]


def make_slope(readings, a16, b16, c16):
    af = a16.astype(jnp.float32)
    cf = c16.astype(jnp.float32)
    scaled = (af[None, :, :] * cf[:, None, :]).astype(jnp.bfloat16)
    model = lax.dot_general(
        scaled, b16, (((2,), (0,)), ((), ())), preferred_element_type=jnp.float32
    )
    slope = ((model - readings.astype(jnp.float32)) / (model * model)).astype(jnp.bfloat16)
    part_second = lax.dot_general(
        scaled, slope, (((0, 1), (0, 1)), ((), ())), preferred_element_type=jnp.float32
    )
    return slope, part_second


def make_cross(slope, a16, b16, c16):
    af = a16.astype(jnp.float32)
    cf = c16.astype(jnp.float32)
    cross = lax.dot_general(
        slope, b16, (((2,), (1,)), ((), ())), preferred_element_type=jnp.float32
    )
    part_first = jnp.sum(cross * cf[:, None, :], axis=0)
    part_time = jnp.sum(cross * af[None, :, :], axis=1)
    return part_first, jnp.pad(part_time, ((0, 16 - part_time.shape[0]), (0, 0)))


def body(
    readings,
    factor_first,
    factor_second,
    factor_time,
    mean_first,
    square_first,
    mean_second,
    square_second,
    mean_time,
    square_time,
):
    ni, nt = lax.axis_size("ia"), lax.axis_size("ta")
    nj = lax.axis_size("zh") * lax.axis_size("co")
    whole_i = readings.shape[1] * ni
    whole_j = readings.shape[2] * nj
    whole_k = readings.shape[0] * nt
    n_time, rank = factor_time.shape
    scale_first = rank / (whole_j * whole_k)
    scale_second = rank / (whole_i * whole_k)
    scale_time = rank / (whole_i * whole_j)
    rows = factor_first.shape[0]
    ranks, cols = factor_second.shape
    flat = 2 * ranks
    zh, ta = lax.axis_index("zh"), lax.axis_index("ta")
    high = zh == 1

    slots, own_first = pack(
        nt,
        (factor_first, mean_first, square_first),
        (factor_second, mean_second, square_second),
    )
    got = lax.all_to_all(slots, "ta", 0, 0)
    wide_second, wide_mean, wide_square = [
        got[:, n * flat : (n + 1) * flat].reshape(nt * flat, rank) for n in (0, 1, 2)
    ]
    a16 = got[:, 3 * flat :].astype(jnp.bfloat16).reshape(nt * rows, rank)

    pad = [a16[n * ranks : (n + 1) * ranks] for n in range(4)]
    slots = spread_slots(wide_second, [jnp.concatenate(pad, axis=1)])
    slots, a16, own_first = lax.optimization_barrier((slots, a16, own_first))
    b16, _ = spread_second(slots, ranks)
    a16 = join_cores(a16[None]).reshape(-1, rank)
    low, up = pick(high, a16, swap(a16, "zh", 1))
    a16 = jnp.concatenate([low, up], axis=0)
    low, up = pick(high, own_first, swap(own_first, "zh", 1))
    pair_first, pair_mean, pair_square = [
        jnp.concatenate([low[n : n + rows], up[n : n + rows]], axis=0)
        for n in (0, rows, 2 * rows)
    ]
    c16 = factor_time.astype(jnp.bfloat16)
    slope, part_second = make_slope(readings, a16, b16, c16)
    slots = second_slots(part_second, ni, [jnp.concatenate(pad, axis=1)])
    slope, slots = lax.optimization_barrier((slope, slots))
    second, _ = sum_second(slots, ranks)
    part_first, part_time = make_cross(slope, a16, b16, c16)
    part, [time_ja] = core_half(part_first, [part_time])
    both = jnp.concatenate([part, time_ja], axis=0)
    both = both + swap(both, "zh", 1)
    part, time_ja = both[: 8 * rows], both[8 * rows :]
    part = part.reshape(2, nt, rows, rank).transpose(1, 0, 2, 3).reshape(nt, 2 * rows, rank)
    second = stack_columns(second)
    slots = jnp.concatenate(
        [part, jnp.broadcast_to(second, (nt,) + second.shape)], axis=1
    )
    got = jnp.sum(lax.all_to_all(slots, "ta", 0, 0), axis=0)
    count = ADAM_STEP + 1
    wide_second, wide_mean, wide_square = adam(
        wide_second, got[2 * rows :] * scale_second, wide_mean, wide_square, count
    )
    pair_first, pair_mean, pair_square = adam(
        pair_first, got[: 2 * rows] * scale_first, pair_mean, pair_square, count
    )

    slots = spread_slots(wide_second, bf16_pair(fold(time_ja, ranks // 2)))
    b16, came = spread_second(slots, ranks)
    a16 = gather_first(pair_first.astype(jnp.bfloat16))
    time_sum = time_of(came, rank)[:n_time]
    factor_time, mean_time, square_time = adam(
        factor_time, time_sum * scale_time, mean_time, square_time, count
    )
    c16 = factor_time.astype(jnp.bfloat16)
    slope, part_second = make_slope(readings, a16, b16, c16)
    part_first, part_time = make_cross(slope, a16, b16, c16)
    second, came = sum_second(
        second_slots(part_second, ni, bf16_pair(fold(part_time, ranks // 2))), ranks
    )
    part, _ = core_half(part_first, [])
    keep, send = pick(high, part[: 4 * rows], part[4 * rows :])
    part = keep + swap(send, "zh", 1)
    time_sum = time_of(came, rank)
    for axis in ("co", "zh"):
        time_sum = time_sum + swap(time_sum, axis, 1)
    slots = jnp.concatenate(
        [part.reshape(nt, rows, rank), stack_columns(second).reshape(nt, flat, rank)], axis=1
    )
    got = jnp.sum(lax.all_to_all(slots, "ta", 0, 0), axis=0)
    count = ADAM_STEP + 2
    first = lambda x: jnp.where(high, x[rows:], x[:rows])
    own = lambda x: unstack_columns(lax.dynamic_slice_in_dim(x, ta * flat, flat, axis=0), ranks)
    factor_first, mean_first, square_first = adam(
        first(pair_first), got[:rows] * scale_first, first(pair_mean), first(pair_square), count
    )
    factor_second, mean_second, square_second = adam(
        own(wide_second),
        unstack_columns(got[rows:], ranks) * scale_second,
        own(wide_mean),
        own(wide_square),
        count,
    )
    factor_time, mean_time, square_time = adam(
        factor_time, time_sum[:n_time] * scale_time, mean_time, square_time, count
    )
    return (
        factor_first,
        factor_second,
        factor_time,
        mean_first,
        square_first,
        mean_second,
        square_second,
        mean_time,
        square_time,
    )


def solution(mesh):
    shape = (mesh.shape["ia"], 2, mesh.shape["ja"] // 2, mesh.shape["ta"])
    mesh = jax.sharding.Mesh(mesh.devices.reshape(shape), ("ia", "zh", "co", "ta"))
    first = P(("ia", "zh", "co", "ta"), None)
    second = P("ia", ("zh", "co", "ta"))
    time = P("ta", None)
    return jax.shard_map(
        body,
        mesh=mesh,
        in_specs=(
            P("ta", "ia", ("zh", "co")),
            first,
            second,
            time,
            first,
            first,
            second,
            second,
            time,
            time,
        ),
        out_specs=(first, second, time, first, first, second, second, time, time),
        check_vma=False,
    )
```

```python
import jax
import jax.numpy as jnp
from jax import lax
from jax.experimental import pallas as pl
from jax.experimental.pallas import tpu as pltpu
from jax.sharding import PartitionSpec as P

ADAM_STEP = 20


beta_one = 0.9
beta_two = 0.99
step_rate = 0.02
tiny_eps = 1e-08


def adam(value, grad, mean, square, count):
    drift = beta_one * mean + (1.0 - beta_one) * grad
    spread = beta_two * square + (1.0 - beta_two) * grad * grad
    fixed_one = 1.0 - beta_one**count
    fixed_two = 1.0 - beta_two**count
    value = value - step_rate * (drift / fixed_one) / (jnp.sqrt(spread / fixed_two) + tiny_eps)
    return (value, drift, spread)


def swap(x, axis, k):
    n = lax.axis_size(axis)
    return lax.ppermute(x, axis, [(i, i ^ k) for i in range(n)])


def pick(flag, x, y):
    return jnp.where(flag, y, x), jnp.where(flag, x, y)


def gather_ta(x):
    ta = lax.axis_index("ta")
    p = [x] + [swap(x, "ta", k) for k in (1, 2, 3)]
    odd, high = (ta & 1) == 1, (ta & 2) == 2
    q0, q1 = pick(odd, p[0], p[1])
    q2, q3 = pick(odd, p[2], p[3])
    q0, q2 = pick(high, q0, q2)
    q1, q3 = pick(high, q1, q3)
    return [q0, q1, q2, q3]


def stack_columns(x):
    return jnp.concatenate([x[:, n * 128 : (n + 1) * 128] for n in range(x.shape[1] // 128)], axis=0)


def unstack_columns(x, ranks):
    return jnp.concatenate([x[n * ranks : (n + 1) * ranks] for n in range(x.shape[0] // ranks)], axis=1)


def pack_kernel(f0, f1, f2, s0, s1, s2, out, state):
    rows = f0.shape[0]
    ranks = s0.shape[0]
    for p in range(out.shape[0]):
        for n, x in enumerate((s0, s1, s2)):
            for h in (0, 1):
                at = (2 * n + h) * ranks
                out[p, at : at + ranks, :] = x[:, h * 128 : (h + 1) * 128]
        out[p, 6 * ranks :, :] = f0[...]
    for n, x in enumerate((f0, f1, f2)):
        state[n * rows : (n + 1) * rows, :] = x[...]


def pack(copies, firsts, seconds):
    rows, rank = firsts[0].shape
    slots = (copies, rows + 6 * seconds[0].shape[0], rank)
    return pl.pallas_call(
        pack_kernel,
        out_shape=[
            jax.ShapeDtypeStruct(slots, jnp.float32),
            jax.ShapeDtypeStruct((3 * rows, rank), jnp.float32),
        ],
        in_specs=[pl.BlockSpec(memory_space=pltpu.VMEM)] * 6,
        out_specs=[pl.BlockSpec(memory_space=pltpu.VMEM)] * 2,
    )(*firsts, *seconds)


def join_cores(x):
    low, high = pick(lax.axis_index("co") == 1, x, swap(x, "co", 1))
    return jnp.stack([low, high], axis=1)


def gather_first(pair):
    rank = pair.shape[1]
    x = join_cores(pair.reshape(2, -1, rank))
    x = x.reshape((-1,) + x.shape[2:])
    return jnp.stack(gather_ta(x), axis=1).reshape(-1, rank)


def core_half(part, extra):
    one = lax.axis_index("co") == 1
    quarter = part.shape[0] // 4
    q = [part[n * quarter : (n + 1) * quarter] for n in range(4)]
    keep0, send0 = pick(one, q[0], q[1])
    keep1, send1 = pick(one, q[2], q[3])
    keep = jnp.concatenate([keep0, keep1], axis=0)
    got = swap(jnp.concatenate([send0, send1] + extra, axis=0), "co", 1)
    half = keep.shape[0]
    return keep + got[:half], [extra[0] + got[half:]] if extra else []


def bf16_pair(x):
    top = lax.reduce_precision(x, 8, 7)
    return [top.astype(jnp.bfloat16), (x - top).astype(jnp.bfloat16)]


def fold(x, rows):
    return jnp.concatenate([x[n * rows : (n + 1) * rows] for n in range(x.shape[0] // rows)], axis=1)


def time_of(got, rank):
    r = got.shape[1] // 2
    line = jnp.sum(got[:, :r].astype(jnp.float32) + got[:, r:].astype(jnp.float32), axis=0)
    return jnp.concatenate(
        [line[:, n * rank : (n + 1) * rank] for n in range(line.shape[1] // rank)], axis=0
    )


def spread_slots(stacked, extra):
    ni = lax.axis_size("ia")
    wide = stacked.astype(jnp.bfloat16)
    half = wide.shape[0] // 2
    ranks = half // 4
    flat = jnp.concatenate(
        [unstack_columns(wide[:half], ranks), unstack_columns(wide[half:], ranks)] + extra, axis=0
    )
    return jnp.broadcast_to(flat, (ni,) + flat.shape)


def spread_second(slots, ranks):
    ni, _, width = slots.shape
    got = lax.all_to_all(slots, "ia", 0, 0)
    b16 = jnp.concatenate(
        [
            got[:, :ranks].reshape(ni * ranks, width),
            got[:, ranks : 2 * ranks].reshape(ni * ranks, width),
        ],
        axis=1,
    )
    return b16, got[:, 2 * ranks :]


def second_slots(part, ni, extra):
    ranks = part.shape[0] // ni
    half = part.shape[1] // 2
    cut = part.astype(jnp.bfloat16).reshape(ni, ranks, 2, half)
    slots = [cut[:, :, 0], cut[:, :, 1]]
    slots += [jnp.broadcast_to(x, (ni,) + x.shape) for x in extra]
    return jnp.concatenate(slots, axis=1)


def sum_second(slots, ranks):
    got = lax.all_to_all(slots, "ia", 0, 0)
    total = jnp.sum(got[:, : 2 * ranks].astype(jnp.float32), axis=0)
    return jnp.concatenate([total[:ranks], total[ranks:]], axis=1), got[:, 2 * ranks :]


def make_slope(readings, a16, b16, c16):
    af = a16.astype(jnp.float32)
    cf = c16.astype(jnp.float32)
    scaled = (af[None, :, :] * cf[:, None, :]).astype(jnp.bfloat16)
    model = lax.dot_general(
        scaled, b16, (((2,), (0,)), ((), ())), preferred_element_type=jnp.float32
    )
    slope = ((model - readings.astype(jnp.float32)) / (model * model)).astype(jnp.bfloat16)
    part_second = lax.dot_general(
        scaled, slope, (((0, 1), (0, 1)), ((), ())), preferred_element_type=jnp.float32
    )
    return slope, part_second


def make_cross(slope, a16, b16, c16):
    af = a16.astype(jnp.float32)
    cf = c16.astype(jnp.float32)
    cross = lax.dot_general(
        slope, b16, (((2,), (1,)), ((), ())), preferred_element_type=jnp.float32
    )
    part_first = jnp.sum(cross * cf[:, None, :], axis=0)
    part_time = jnp.sum(cross * af[None, :, :], axis=1)
    return part_first, jnp.pad(part_time, ((0, 16 - part_time.shape[0]), (0, 0)))


def body(
    readings,
    factor_first,
    factor_second,
    factor_time,
    mean_first,
    square_first,
    mean_second,
    square_second,
    mean_time,
    square_time,
):
    ni, nt = lax.axis_size("ia"), lax.axis_size("ta")
    nj = lax.axis_size("zh") * lax.axis_size("co")
    whole_i = readings.shape[1] * ni
    whole_j = readings.shape[2] * nj
    whole_k = readings.shape[0] * nt
    n_time, rank = factor_time.shape
    scale_first = rank / (whole_j * whole_k)
    scale_second = rank / (whole_i * whole_k)
    scale_time = rank / (whole_i * whole_j)
    rows = factor_first.shape[0]
    ranks, cols = factor_second.shape
    flat = 2 * ranks
    zh, ta = lax.axis_index("zh"), lax.axis_index("ta")
    high = zh == 1

    slots, own_first = pack(
        nt,
        (factor_first, mean_first, square_first),
        (factor_second, mean_second, square_second),
    )
    got = lax.all_to_all(slots, "ta", 0, 0)
    wide_second, wide_mean, wide_square = [
        got[:, n * flat : (n + 1) * flat].reshape(nt * flat, rank) for n in (0, 1, 2)
    ]
    a16 = got[:, 3 * flat :].astype(jnp.bfloat16).reshape(nt * rows, rank)

    pad = [a16[n * ranks : (n + 1) * ranks] for n in range(4)]
    slots = spread_slots(wide_second, [jnp.concatenate(pad, axis=1)])
    slots, a16 = lax.optimization_barrier((slots, a16))
    b16, _ = spread_second(slots, ranks)
    a16 = join_cores(a16[None]).reshape(-1, rank)
    low, up = pick(high, a16, swap(a16, "zh", 1))
    a16 = jnp.concatenate([low, up], axis=0)
    c16 = factor_time.astype(jnp.bfloat16)
    slope, part_second = make_slope(readings, a16, b16, c16)
    part_first, part_time = make_cross(slope, a16, b16, c16)
    second, _ = sum_second(second_slots(part_second, ni, []), ranks)
    part, [part_time] = core_half(part_first, [part_time])
    sent = jnp.concatenate([part, part_time, own_first], axis=0)
    came = swap(sent, "zh", 1)
    low, up = pick(high, own_first, came[9 * rows :])
    pair_first, pair_mean, pair_square = [
        jnp.concatenate([low[n : n + rows], up[n : n + rows]], axis=0)
        for n in (0, rows, 2 * rows)
    ]
    part = part + came[: 8 * rows]
    time_ja = part_time + came[8 * rows : 9 * rows]
    part = part.reshape(2, nt, rows, rank).transpose(1, 0, 2, 3).reshape(nt, 2 * rows, rank)
    second = stack_columns(second)
    slot = lambda t: jnp.concatenate(
        [lax.dynamic_index_in_dim(part, t, 0, keepdims=False), second], axis=0
    )
    got = [slot(ta)] + [swap(slot(ta ^ k), "ta", k) for k in (1, 2, 3)]
    got = (got[0] + got[1]) + (got[2] + got[3])
    grad_first, grad_second = got[: 2 * rows], got[2 * rows :]
    count = ADAM_STEP + 1
    wide_second, wide_mean, wide_square = adam(
        wide_second, grad_second * scale_second, wide_mean, wide_square, count
    )
    pair_first, pair_mean, pair_square = adam(
        pair_first, grad_first * scale_first, pair_mean, pair_square, count
    )

    slots = spread_slots(wide_second, bf16_pair(fold(time_ja, ranks // 2)))
    b16, came = spread_second(slots, ranks)
    a16 = gather_first(pair_first.astype(jnp.bfloat16))
    time_sum = time_of(came, rank)[:n_time]
    factor_time, mean_time, square_time = adam(
        factor_time, time_sum * scale_time, mean_time, square_time, count
    )
    c16 = factor_time.astype(jnp.bfloat16)
    slope, part_second = make_slope(readings, a16, b16, c16)
    part_first, part_time = make_cross(slope, a16, b16, c16)
    part, [part_time] = core_half(part_first, [part_time])
    second, came = sum_second(
        second_slots(part_second, ni, bf16_pair(fold(part_time, ranks // 2))), ranks
    )
    keep, send = pick(high, part[: 4 * rows], part[4 * rows :])
    part = keep + swap(send, "zh", 1)
    time_sum = time_of(came, rank)
    time_sum = time_sum + swap(time_sum, "zh", 1)
    slots = jnp.concatenate(
        [part.reshape(nt, rows, rank), stack_columns(second).reshape(nt, flat, rank)], axis=1
    )
    slot = lambda t: lax.dynamic_index_in_dim(slots, t, 0, keepdims=False)
    got = [slot(ta)] + [swap(slot(ta ^ k), "ta", k) for k in (1, 2, 3)]
    got = (got[0] + got[1]) + (got[2] + got[3])
    count = ADAM_STEP + 2
    first = lambda x: jnp.where(high, x[rows:], x[:rows])
    own = lambda x: unstack_columns(lax.dynamic_slice_in_dim(x, ta * flat, flat, axis=0), ranks)
    factor_first, mean_first, square_first = adam(
        first(pair_first), got[:rows] * scale_first, first(pair_mean), first(pair_square), count
    )
    factor_second, mean_second, square_second = adam(
        own(wide_second),
        unstack_columns(got[rows:], ranks) * scale_second,
        own(wide_mean),
        own(wide_square),
        count,
    )
    factor_time, mean_time, square_time = adam(
        factor_time, time_sum[:n_time] * scale_time, mean_time, square_time, count
    )
    return (
        factor_first,
        factor_second,
        factor_time,
        mean_first,
        square_first,
        mean_second,
        square_second,
        mean_time,
        square_time,
    )


def solution(mesh):
    shape = (mesh.shape["ia"], 2, mesh.shape["ja"] // 2, mesh.shape["ta"])
    mesh = jax.sharding.Mesh(mesh.devices.reshape(shape), ("ia", "zh", "co", "ta"))
    first = P(("ia", "zh", "co", "ta"), None)
    second = P("ia", ("zh", "co", "ta"))
    time = P("ta", None)
    return jax.shard_map(
        body,
        mesh=mesh,
        in_specs=(
            P("ta", "ia", ("zh", "co")),
            first,
            second,
            time,
            first,
            first,
            second,
            second,
            time,
            time,
        ),
        out_specs=(first, second, time, first, first, second, second, time, time),
        check_vma=False,
    )
```

```python
import jax
import jax.numpy as jnp
from jax import lax
from jax.experimental import pallas as pl
from jax.experimental.pallas import tpu as pltpu
from jax.sharding import PartitionSpec as P

ADAM_STEP = 20


beta_one = 0.9
beta_two = 0.99
step_rate = 0.02
tiny_eps = 1e-08


def adam(value, grad, mean, square, count):
    drift = beta_one * mean + (1.0 - beta_one) * grad
    spread = beta_two * square + (1.0 - beta_two) * grad * grad
    fixed_one = 1.0 - beta_one**count
    fixed_two = 1.0 - beta_two**count
    value = value - step_rate * (drift / fixed_one) / (jnp.sqrt(spread / fixed_two) + tiny_eps)
    return (value, drift, spread)


def swap(x, axis, k):
    n = lax.axis_size(axis)
    return lax.ppermute(x, axis, [(i, i ^ k) for i in range(n)])


def pick(flag, x, y):
    return jnp.where(flag, y, x), jnp.where(flag, x, y)


def gather_ta(x):
    ta = lax.axis_index("ta")
    p = [x] + [swap(x, "ta", k) for k in (1, 2, 3)]
    odd, high = (ta & 1) == 1, (ta & 2) == 2
    q0, q1 = pick(odd, p[0], p[1])
    q2, q3 = pick(odd, p[2], p[3])
    q0, q2 = pick(high, q0, q2)
    q1, q3 = pick(high, q1, q3)
    return [q0, q1, q2, q3]


def stack_columns(x):
    return jnp.concatenate([x[:, n * 128 : (n + 1) * 128] for n in range(x.shape[1] // 128)], axis=0)


def unstack_columns(x, ranks):
    return jnp.concatenate([x[n * ranks : (n + 1) * ranks] for n in range(x.shape[0] // ranks)], axis=1)


def pack_kernel(f0, f1, f2, s0, s1, s2, out, state):
    rows = f0.shape[0]
    ranks = s0.shape[0]
    for p in range(out.shape[0]):
        for n, x in enumerate((s0, s1, s2)):
            for h in (0, 1):
                at = (2 * n + h) * ranks
                out[p, at : at + ranks, :] = x[:, h * 128 : (h + 1) * 128]
        out[p, 6 * ranks :, :] = f0[...]
    for n, x in enumerate((f0, f1, f2)):
        state[n * rows : (n + 1) * rows, :] = x[...]


def pack(copies, firsts, seconds):
    rows, rank = firsts[0].shape
    slots = (copies, rows + 6 * seconds[0].shape[0], rank)
    return pl.pallas_call(
        pack_kernel,
        out_shape=[
            jax.ShapeDtypeStruct(slots, jnp.float32),
            jax.ShapeDtypeStruct((3 * rows, rank), jnp.float32),
        ],
        in_specs=[pl.BlockSpec(memory_space=pltpu.VMEM)] * 6,
        out_specs=[pl.BlockSpec(memory_space=pltpu.VMEM)] * 2,
    )(*firsts, *seconds)


def join_cores(x):
    low, high = pick(lax.axis_index("co") == 1, x, swap(x, "co", 1))
    return jnp.stack([low, high], axis=1)


def gather_first(pair):
    rank = pair.shape[1]
    x = join_cores(pair.reshape(2, -1, rank))
    x = x.reshape((-1,) + x.shape[2:])
    return jnp.stack(gather_ta(x), axis=1).reshape(-1, rank)


def core_half(part, extra):
    one = lax.axis_index("co") == 1
    quarter = part.shape[0] // 4
    q = [part[n * quarter : (n + 1) * quarter] for n in range(4)]
    keep0, send0 = pick(one, q[0], q[1])
    keep1, send1 = pick(one, q[2], q[3])
    keep = jnp.concatenate([keep0, keep1], axis=0)
    got = swap(jnp.concatenate([send0, send1] + extra, axis=0), "co", 1)
    half = keep.shape[0]
    return keep + got[:half], [extra[0] + got[half:]] if extra else []


def bf16_pair(x):
    top = lax.reduce_precision(x, 8, 7)
    return [top.astype(jnp.bfloat16), (x - top).astype(jnp.bfloat16)]


def fold(x, rows):
    return jnp.concatenate([x[n * rows : (n + 1) * rows] for n in range(x.shape[0] // rows)], axis=1)


def time_of(got, rank):
    r = got.shape[1] // 2
    line = jnp.sum(got[:, :r].astype(jnp.float32) + got[:, r:].astype(jnp.float32), axis=0)
    return jnp.concatenate(
        [line[:, n * rank : (n + 1) * rank] for n in range(line.shape[1] // rank)], axis=0
    )


def spread_slots(stacked, extra):
    ni = lax.axis_size("ia")
    wide = stacked.astype(jnp.bfloat16)
    half = wide.shape[0] // 2
    ranks = half // 4
    flat = jnp.concatenate(
        [unstack_columns(wide[:half], ranks), unstack_columns(wide[half:], ranks)] + extra, axis=0
    )
    return jnp.broadcast_to(flat, (ni,) + flat.shape)


def spread_second(slots, ranks):
    ni, _, width = slots.shape
    got = lax.all_to_all(slots, "ia", 0, 0)
    b16 = jnp.concatenate(
        [
            got[:, :ranks].reshape(ni * ranks, width),
            got[:, ranks : 2 * ranks].reshape(ni * ranks, width),
        ],
        axis=1,
    )
    return b16, got[:, 2 * ranks :]


def sum_second(slots, ranks):
    got = lax.all_to_all(slots, "ia", 0, 0)
    total = jnp.sum(got[:, : 2 * ranks].astype(jnp.float32), axis=0)
    return jnp.concatenate([total[:ranks], total[ranks:]], axis=1), got[:, 2 * ranks :]


def step_kernel(readings, a16, b16, times, part_first, slots, part_time, total):
    block = readings.shape[0]
    now = pl.program_id(0)
    af = a16[...].astype(jnp.float32)
    bf = b16[...]

    @pl.when(now == 0)
    def _():
        total[...] = jnp.zeros_like(total)
        part_first[...] = jnp.zeros_like(part_first)
        part_time[...] = jnp.zeros_like(part_time)

    row = lax.broadcasted_iota(jnp.int32, part_time.shape, 0)
    first, time = part_first[...], part_time[...]
    all_scaled, all_slope = [], []
    for t in range(block):
        cf = times[now * block + t]
        scaled = (af * cf).astype(jnp.bfloat16)
        model = jnp.dot(scaled, bf, preferred_element_type=jnp.float32)
        inverse = 1.0 / model
        slope = inverse * (1.0 - readings[t].astype(jnp.float32) * inverse)
        slope = slope.astype(jnp.bfloat16)
        cross = lax.dot_general(
            slope, bf, (((1,), (1,)), ((), ())), preferred_element_type=jnp.float32
        )
        first = first + cross * cf
        line = jnp.sum(cross * af, axis=0, keepdims=True)
        time = time + jnp.where(row == now * block + t, line, 0.0)
        all_scaled.append(scaled)
        all_slope.append(slope)
    part_first[...] = first
    part_time[...] = time
    total[...] += lax.dot_general(
        jnp.concatenate(all_scaled, axis=0),
        jnp.concatenate(all_slope, axis=0),
        (((0,), (0,)), ((), ())),
        preferred_element_type=jnp.float32,
    )

    @pl.when(now == pl.num_programs(0) - 1)
    def _():
        count = slots.shape[0]
        ranks = total.shape[0] // count
        half = total.shape[1] // 2
        for p in range(count):
            rows = total[p * ranks : (p + 1) * ranks, :]
            flat = jnp.concatenate([rows[:, :half], rows[:, half:]], axis=0)
            slots[p] = flat.astype(slots.dtype)


def step_parts(readings, a16, b16, c16, ni):
    times, rows, cols = readings.shape
    rank = a16.shape[1]
    block = 4
    return pl.pallas_call(
        step_kernel,
        grid=(times // block,),
        in_specs=[
            pl.BlockSpec((block, rows, cols), lambda k: (k, 0, 0)),
            pl.BlockSpec((rows, rank), lambda k: (0, 0)),
            pl.BlockSpec((rank, cols), lambda k: (0, 0)),
            pl.BlockSpec((times, 1, rank), lambda k: (0, 0, 0)),
        ],
        out_specs=[
            pl.BlockSpec((rows, rank), lambda k: (0, 0)),
            pl.BlockSpec((ni, 2 * rank // ni, cols // 2), lambda k: (0, 0, 0)),
            pl.BlockSpec((16, rank), lambda k: (0, 0)),
        ],
        out_shape=[
            jax.ShapeDtypeStruct((rows, rank), jnp.float32),
            jax.ShapeDtypeStruct((ni, 2 * rank // ni, cols // 2), jnp.bfloat16),
            jax.ShapeDtypeStruct((16, rank), jnp.float32),
        ],
        scratch_shapes=[pltpu.VMEM((rank, cols), jnp.float32)],
        compiler_params=pltpu.CompilerParams(vmem_limit_bytes=50 * 2**20),
        cost_estimate=pl.CostEstimate(
            flops=6 * times * rows * cols * rank,
            bytes_accessed=2 * times * rows * cols,
            transcendentals=times * rows * cols,
        ),
    )(readings, a16, b16, c16.astype(jnp.float32)[:, None, :])


def body(
    readings,
    factor_first,
    factor_second,
    factor_time,
    mean_first,
    square_first,
    mean_second,
    square_second,
    mean_time,
    square_time,
):
    ni, nt = lax.axis_size("ia"), lax.axis_size("ta")
    nj = lax.axis_size("zh") * lax.axis_size("co")
    whole_i = readings.shape[1] * ni
    whole_j = readings.shape[2] * nj
    whole_k = readings.shape[0] * nt
    n_time, rank = factor_time.shape
    scale_first = rank / (whole_j * whole_k)
    scale_second = rank / (whole_i * whole_k)
    scale_time = rank / (whole_i * whole_j)
    rows = factor_first.shape[0]
    ranks, cols = factor_second.shape
    flat = 2 * ranks
    zh, ta = lax.axis_index("zh"), lax.axis_index("ta")
    high = zh == 1

    slots, own_first = pack(
        nt,
        (factor_first, mean_first, square_first),
        (factor_second, mean_second, square_second),
    )
    got = lax.all_to_all(slots, "ta", 0, 0)
    wide_second, wide_mean, wide_square = [
        got[:, n * flat : (n + 1) * flat].reshape(nt * flat, rank) for n in (0, 1, 2)
    ]
    a16 = got[:, 3 * flat :].astype(jnp.bfloat16).reshape(nt * rows, rank)

    pad = [a16[n * ranks : (n + 1) * ranks] for n in range(4)]
    slots = spread_slots(wide_second, [jnp.concatenate(pad, axis=1)])
    slots, a16 = lax.optimization_barrier((slots, a16))
    b16, _ = spread_second(slots, ranks)
    a16 = join_cores(a16[None]).reshape(-1, rank)
    low, up = pick(high, a16, swap(a16, "zh", 1))
    a16 = jnp.concatenate([low, up], axis=0)
    c16 = factor_time.astype(jnp.bfloat16)
    part_first, slots, part_time = step_parts(readings, a16, b16, c16, ni)
    second, _ = sum_second(slots, ranks)
    part, [part_time] = core_half(part_first, [part_time])
    sent = jnp.concatenate([part, part_time, own_first], axis=0)
    came = swap(sent, "zh", 1)
    low, up = pick(high, own_first, came[9 * rows :])
    pair_first, pair_mean, pair_square = [
        jnp.concatenate([low[n : n + rows], up[n : n + rows]], axis=0)
        for n in (0, rows, 2 * rows)
    ]
    part = part + came[: 8 * rows]
    time_ja = part_time + came[8 * rows : 9 * rows]
    part = part.reshape(2, nt, rows, rank).transpose(1, 0, 2, 3).reshape(nt, 2 * rows, rank)
    second = stack_columns(second)
    slot = lambda t: jnp.concatenate(
        [lax.dynamic_index_in_dim(part, t, 0, keepdims=False), second], axis=0
    )
    got = [slot(ta)] + [swap(slot(ta ^ k), "ta", k) for k in (1, 2, 3)]
    got = (got[0] + got[1]) + (got[2] + got[3])
    grad_first, grad_second = got[: 2 * rows], got[2 * rows :]
    count = ADAM_STEP + 1
    wide_second, wide_mean, wide_square = adam(
        wide_second, grad_second * scale_second, wide_mean, wide_square, count
    )
    pair_first, pair_mean, pair_square = adam(
        pair_first, grad_first * scale_first, pair_mean, pair_square, count
    )

    slots = spread_slots(wide_second, bf16_pair(fold(time_ja, ranks // 2)))
    b16, came = spread_second(slots, ranks)
    a16 = gather_first(pair_first.astype(jnp.bfloat16))
    time_sum = time_of(came, rank)[:n_time]
    factor_time, mean_time, square_time = adam(
        factor_time, time_sum * scale_time, mean_time, square_time, count
    )
    c16 = factor_time.astype(jnp.bfloat16)
    part_first, slots, part_time = step_parts(readings, a16, b16, c16, ni)
    part, [part_time] = core_half(part_first, [part_time])
    line = jnp.concatenate(bf16_pair(fold(part_time, ranks // 2)), axis=0)
    line = jnp.broadcast_to(line, (ni,) + line.shape)
    second, came = sum_second(jnp.concatenate([slots, line], axis=1), ranks)
    keep, send = pick(high, part[: 4 * rows], part[4 * rows :])
    part = keep + swap(send, "zh", 1)
    time_sum = time_of(came, rank)
    time_sum = time_sum + swap(time_sum, "zh", 1)
    slots = jnp.concatenate(
        [part.reshape(nt, rows, rank), stack_columns(second).reshape(nt, flat, rank)], axis=1
    )
    slot = lambda t: lax.dynamic_index_in_dim(slots, t, 0, keepdims=False)
    got = [slot(ta)] + [swap(slot(ta ^ k), "ta", k) for k in (1, 2, 3)]
    got = (got[0] + got[1]) + (got[2] + got[3])
    count = ADAM_STEP + 2
    first = lambda x: jnp.where(high, x[rows:], x[:rows])
    own = lambda x: unstack_columns(lax.dynamic_slice_in_dim(x, ta * flat, flat, axis=0), ranks)
    factor_first, mean_first, square_first = adam(
        first(pair_first), got[:rows] * scale_first, first(pair_mean), first(pair_square), count
    )
    factor_second, mean_second, square_second = adam(
        own(wide_second),
        unstack_columns(got[rows:], ranks) * scale_second,
        own(wide_mean),
        own(wide_square),
        count,
    )
    factor_time, mean_time, square_time = adam(
        factor_time, time_sum[:n_time] * scale_time, mean_time, square_time, count
    )
    return (
        factor_first,
        factor_second,
        factor_time,
        mean_first,
        square_first,
        mean_second,
        square_second,
        mean_time,
        square_time,
    )


def solution(mesh):
    shape = (mesh.shape["ia"], 2, mesh.shape["ja"] // 2, mesh.shape["ta"])
    mesh = jax.sharding.Mesh(mesh.devices.reshape(shape), ("ia", "zh", "co", "ta"))
    first = P(("ia", "zh", "co", "ta"), None)
    second = P("ia", ("zh", "co", "ta"))
    time = P("ta", None)
    return jax.shard_map(
        body,
        mesh=mesh,
        in_specs=(
            P("ta", "ia", ("zh", "co")),
            first,
            second,
            time,
            first,
            first,
            second,
            second,
            time,
            time,
        ),
        out_specs=(first, second, time, first, first, second, second, time, time),
        check_vma=False,
    )
```

```python
import jax
import jax.numpy as jnp
from jax import lax
from jax.experimental import pallas as pl
from jax.experimental.pallas import tpu as pltpu
from jax.sharding import PartitionSpec as P

ADAM_STEP = 20


beta_one = 0.9
beta_two = 0.99
step_rate = 0.02
tiny_eps = 1e-08


def adam(value, grad, mean, square, count):
    drift = beta_one * mean + (1.0 - beta_one) * grad
    spread = beta_two * square + (1.0 - beta_two) * grad * grad
    fixed_one = 1.0 - beta_one**count
    fixed_two = 1.0 - beta_two**count
    value = value - step_rate * (drift / fixed_one) / (jnp.sqrt(spread / fixed_two) + tiny_eps)
    return (value, drift, spread)


def swap(x, axis, k):
    n = lax.axis_size(axis)
    return lax.ppermute(x, axis, [(i, i ^ k) for i in range(n)])


def pick(flag, x, y):
    return jnp.where(flag, y, x), jnp.where(flag, x, y)


def gather_ta(x):
    ta = lax.axis_index("ta")
    p = [x] + [swap(x, "ta", k) for k in (1, 2, 3)]
    odd, high = (ta & 1) == 1, (ta & 2) == 2
    q0, q1 = pick(odd, p[0], p[1])
    q2, q3 = pick(odd, p[2], p[3])
    q0, q2 = pick(high, q0, q2)
    q1, q3 = pick(high, q1, q3)
    return [q0, q1, q2, q3]


def stack_columns(x):
    return jnp.concatenate([x[:, n * 128 : (n + 1) * 128] for n in range(x.shape[1] // 128)], axis=0)


def unstack_columns(x, ranks):
    return jnp.concatenate([x[n * ranks : (n + 1) * ranks] for n in range(x.shape[0] // ranks)], axis=1)


def pack_kernel(f0, f1, f2, s0, s1, s2, out, state):
    rows = f0.shape[0]
    ranks = s0.shape[0]
    for p in range(out.shape[0]):
        for n, x in enumerate((s0, s1, s2)):
            for h in (0, 1):
                at = (2 * n + h) * ranks
                out[p, at : at + ranks, :] = x[:, h * 128 : (h + 1) * 128]
        out[p, 6 * ranks :, :] = f0[...]
    for n, x in enumerate((f0, f1, f2)):
        state[n * rows : (n + 1) * rows, :] = x[...]


def pack(copies, firsts, seconds):
    rows, rank = firsts[0].shape
    slots = (copies, rows + 6 * seconds[0].shape[0], rank)
    return pl.pallas_call(
        pack_kernel,
        out_shape=[
            jax.ShapeDtypeStruct(slots, jnp.float32),
            jax.ShapeDtypeStruct((3 * rows, rank), jnp.float32),
        ],
        in_specs=[pl.BlockSpec(memory_space=pltpu.VMEM)] * 6,
        out_specs=[pl.BlockSpec(memory_space=pltpu.VMEM)] * 2,
    )(*firsts, *seconds)


def join_cores(x):
    low, high = pick(lax.axis_index("co") == 1, x, swap(x, "co", 1))
    return jnp.stack([low, high], axis=1)


def gather_first(pair):
    rank = pair.shape[1]
    x = join_cores(pair.reshape(2, -1, rank))
    x = x.reshape((-1,) + x.shape[2:])
    return jnp.stack(gather_ta(x), axis=1).reshape(-1, rank)


def core_half(part, extra):
    one = lax.axis_index("co") == 1
    quarter = part.shape[0] // 4
    q = [part[n * quarter : (n + 1) * quarter] for n in range(4)]
    keep0, send0 = pick(one, q[0], q[1])
    keep1, send1 = pick(one, q[2], q[3])
    keep = jnp.concatenate([keep0, keep1], axis=0)
    got = swap(jnp.concatenate([send0, send1] + extra, axis=0), "co", 1)
    half = keep.shape[0]
    return keep + got[:half], [extra[0] + got[half:]] if extra else []


def bf16_pair(x):
    top = lax.reduce_precision(x, 8, 7)
    return [top.astype(jnp.bfloat16), (x - top).astype(jnp.bfloat16)]


def fold(x, rows):
    return jnp.concatenate([x[n * rows : (n + 1) * rows] for n in range(x.shape[0] // rows)], axis=1)


def time_of(got, rank):
    r = got.shape[1] // 2
    line = jnp.sum(got[:, :r].astype(jnp.float32) + got[:, r:].astype(jnp.float32), axis=0)
    return jnp.concatenate(
        [line[:, n * rank : (n + 1) * rank] for n in range(line.shape[1] // rank)], axis=0
    )


def spread_slots(stacked, extra):
    ni = lax.axis_size("ia")
    wide = stacked.astype(jnp.bfloat16)
    half = wide.shape[0] // 2
    ranks = half // 4
    flat = jnp.concatenate(
        [unstack_columns(wide[:half], ranks), unstack_columns(wide[half:], ranks)] + extra, axis=0
    )
    return jnp.broadcast_to(flat, (ni,) + flat.shape)


def spread_second(slots, ranks):
    ni, _, width = slots.shape
    got = lax.all_to_all(slots, "ia", 0, 0)
    b16 = jnp.concatenate(
        [
            got[:, :ranks].reshape(ni * ranks, width),
            got[:, ranks : 2 * ranks].reshape(ni * ranks, width),
        ],
        axis=1,
    )
    return b16, got[:, 2 * ranks :]


def sum_second(slots, ranks):
    got = lax.all_to_all(slots, "ia", 0, 0)
    total = jnp.sum(got[:, : 2 * ranks].astype(jnp.float32), axis=0)
    return jnp.concatenate([total[:ranks], total[ranks:]], axis=1), got[:, 2 * ranks :]


def step_kernel(readings, a16, b16, times, part_first, slots, part_time, total):
    block = readings.shape[0]
    now = pl.program_id(0)
    af = a16[...].astype(jnp.float32)
    bf = b16[...]

    @pl.when(now == 0)
    def _():
        total[...] = jnp.zeros_like(total)
        part_first[...] = jnp.zeros_like(part_first)
        part_time[...] = jnp.zeros_like(part_time)

    row = lax.broadcasted_iota(jnp.int32, part_time.shape, 0)
    first, time = part_first[...], part_time[...]
    all_scaled, all_slope = [], []
    for t in range(block):
        cf = times[now * block + t]
        scaled = (af * cf).astype(jnp.bfloat16)
        model = jnp.dot(scaled, bf, preferred_element_type=jnp.float32)
        inverse = 1.0 / model
        slope = inverse * (1.0 - readings[t].astype(jnp.float32) * inverse)
        slope = slope.astype(jnp.bfloat16)
        cross = lax.dot_general(
            slope, bf, (((1,), (1,)), ((), ())), preferred_element_type=jnp.float32
        )
        first = first + cross * cf
        line = jnp.sum(cross * af, axis=0, keepdims=True)
        time = time + jnp.where(row == now * block + t, line, 0.0)
        all_scaled.append(scaled)
        all_slope.append(slope)
    part_first[...] = first
    part_time[...] = time
    total[...] += lax.dot_general(
        jnp.concatenate(all_scaled, axis=0),
        jnp.concatenate(all_slope, axis=0),
        (((0,), (0,)), ((), ())),
        preferred_element_type=jnp.float32,
    )

    @pl.when(now == pl.num_programs(0) - 1)
    def _():
        count = slots.shape[0]
        ranks = total.shape[0] // count
        half = total.shape[1] // 2
        for p in range(count):
            rows = total[p * ranks : (p + 1) * ranks, :]
            flat = jnp.concatenate([rows[:, :half], rows[:, half:]], axis=0)
            slots[p] = flat.astype(slots.dtype)


def step_parts(readings, a16, b16, c16, ni):
    times, rows, cols = readings.shape
    rank = a16.shape[1]
    block = 4
    return pl.pallas_call(
        step_kernel,
        grid=(times // block,),
        in_specs=[
            pl.BlockSpec((block, rows, cols), lambda k: (k, 0, 0)),
            pl.BlockSpec((rows, rank), lambda k: (0, 0)),
            pl.BlockSpec((rank, cols), lambda k: (0, 0)),
            pl.BlockSpec((times, 1, rank), lambda k: (0, 0, 0)),
        ],
        out_specs=[
            pl.BlockSpec((rows, rank), lambda k: (0, 0)),
            pl.BlockSpec((ni, 2 * rank // ni, cols // 2), lambda k: (0, 0, 0)),
            pl.BlockSpec((16, rank), lambda k: (0, 0)),
        ],
        out_shape=[
            jax.ShapeDtypeStruct((rows, rank), jnp.float32),
            jax.ShapeDtypeStruct((ni, 2 * rank // ni, cols // 2), jnp.bfloat16),
            jax.ShapeDtypeStruct((16, rank), jnp.float32),
        ],
        scratch_shapes=[pltpu.VMEM((rank, cols), jnp.float32)],
        compiler_params=pltpu.CompilerParams(vmem_limit_bytes=50 * 2**20),
        cost_estimate=pl.CostEstimate(
            flops=6 * times * rows * cols * rank,
            bytes_accessed=2 * times * rows * cols,
            transcendentals=times * rows * cols,
        ),
    )(readings, a16, b16, c16.astype(jnp.float32)[:, None, :])


def body(
    readings,
    factor_first,
    factor_second,
    factor_time,
    mean_first,
    square_first,
    mean_second,
    square_second,
    mean_time,
    square_time,
):
    ni, nt = lax.axis_size("ia"), lax.axis_size("ta")
    nj = lax.axis_size("zh") * lax.axis_size("co")
    whole_i = readings.shape[1] * ni
    whole_j = readings.shape[2] * nj
    whole_k = readings.shape[0] * nt
    n_time, rank = factor_time.shape
    scale_first = rank / (whole_j * whole_k)
    scale_second = rank / (whole_i * whole_k)
    scale_time = rank / (whole_i * whole_j)
    rows = factor_first.shape[0]
    ranks, cols = factor_second.shape
    flat = 2 * ranks
    zh, ta = lax.axis_index("zh"), lax.axis_index("ta")
    high = zh == 1

    slots, own_first = pack(
        1,
        (factor_first, mean_first, square_first),
        (factor_second, mean_second, square_second),
    )
    got = jnp.stack(gather_ta(slots[0]), axis=0)
    wide_second, wide_mean, wide_square = [
        got[:, n * flat : (n + 1) * flat].reshape(nt * flat, rank) for n in (0, 1, 2)
    ]
    a16 = got[:, 3 * flat :].astype(jnp.bfloat16).reshape(nt * rows, rank)

    pad = [a16[n * ranks : (n + 1) * ranks] for n in range(4)]
    slots = spread_slots(wide_second, [jnp.concatenate(pad, axis=1)])
    slots, a16 = lax.optimization_barrier((slots, a16))
    b16, _ = spread_second(slots, ranks)
    a16 = join_cores(a16[None]).reshape(-1, rank)
    low, up = pick(high, a16, swap(a16, "zh", 1))
    a16 = jnp.concatenate([low, up], axis=0)
    c16 = factor_time.astype(jnp.bfloat16)
    part_first, slots, part_time = step_parts(readings, a16, b16, c16, ni)
    second, _ = sum_second(slots, ranks)
    part, [part_time] = core_half(part_first, [part_time])
    sent = jnp.concatenate([part, part_time, own_first], axis=0)
    came = swap(sent, "zh", 1)
    low, up = pick(high, own_first, came[9 * rows :])
    pair_first, pair_mean, pair_square = [
        jnp.concatenate([low[n : n + rows], up[n : n + rows]], axis=0)
        for n in (0, rows, 2 * rows)
    ]
    part = part + came[: 8 * rows]
    time_ja = part_time + came[8 * rows : 9 * rows]
    part = part.reshape(2, nt, rows, rank).transpose(1, 0, 2, 3).reshape(nt, 2 * rows, rank)
    second = stack_columns(second)
    slot = lambda t: jnp.concatenate(
        [lax.dynamic_index_in_dim(part, t, 0, keepdims=False), second], axis=0
    )
    got = [slot(ta)] + [swap(slot(ta ^ k), "ta", k) for k in (1, 2, 3)]
    got = (got[0] + got[1]) + (got[2] + got[3])
    grad_first, grad_second = got[: 2 * rows], got[2 * rows :]
    count = ADAM_STEP + 1
    wide_second, wide_mean, wide_square = adam(
        wide_second, grad_second * scale_second, wide_mean, wide_square, count
    )
    pair_first, pair_mean, pair_square = adam(
        pair_first, grad_first * scale_first, pair_mean, pair_square, count
    )

    slots = spread_slots(wide_second, bf16_pair(fold(time_ja, ranks // 2)))
    b16, came = spread_second(slots, ranks)
    a16 = gather_first(pair_first.astype(jnp.bfloat16))
    time_sum = time_of(came, rank)[:n_time]
    factor_time, mean_time, square_time = adam(
        factor_time, time_sum * scale_time, mean_time, square_time, count
    )
    c16 = factor_time.astype(jnp.bfloat16)
    part_first, slots, part_time = step_parts(readings, a16, b16, c16, ni)
    part, [part_time] = core_half(part_first, [part_time])
    line = jnp.concatenate(bf16_pair(fold(part_time, ranks // 2)), axis=0)
    line = jnp.broadcast_to(line, (ni,) + line.shape)
    second, came = sum_second(jnp.concatenate([slots, line], axis=1), ranks)
    keep, send = pick(high, part[: 4 * rows], part[4 * rows :])
    part = keep + swap(send, "zh", 1)
    time_sum = time_of(came, rank)
    time_sum = time_sum + swap(time_sum, "zh", 1)
    slots = jnp.concatenate(
        [part.reshape(nt, rows, rank), stack_columns(second).reshape(nt, flat, rank)], axis=1
    )
    slot = lambda t: lax.dynamic_index_in_dim(slots, t, 0, keepdims=False)
    got = [slot(ta)] + [swap(slot(ta ^ k), "ta", k) for k in (1, 2, 3)]
    got = (got[0] + got[1]) + (got[2] + got[3])
    count = ADAM_STEP + 2
    first = lambda x: jnp.where(high, x[rows:], x[:rows])
    own = lambda x: unstack_columns(lax.dynamic_slice_in_dim(x, ta * flat, flat, axis=0), ranks)
    factor_first, mean_first, square_first = adam(
        first(pair_first), got[:rows] * scale_first, first(pair_mean), first(pair_square), count
    )
    factor_second, mean_second, square_second = adam(
        own(wide_second),
        unstack_columns(got[rows:], ranks) * scale_second,
        own(wide_mean),
        own(wide_square),
        count,
    )
    factor_time, mean_time, square_time = adam(
        factor_time, time_sum[:n_time] * scale_time, mean_time, square_time, count
    )
    return (
        factor_first,
        factor_second,
        factor_time,
        mean_first,
        square_first,
        mean_second,
        square_second,
        mean_time,
        square_time,
    )


def solution(mesh):
    shape = (mesh.shape["ia"], 2, mesh.shape["ja"] // 2, mesh.shape["ta"])
    mesh = jax.sharding.Mesh(mesh.devices.reshape(shape), ("ia", "zh", "co", "ta"))
    first = P(("ia", "zh", "co", "ta"), None)
    second = P("ia", ("zh", "co", "ta"))
    time = P("ta", None)
    return jax.shard_map(
        body,
        mesh=mesh,
        in_specs=(
            P("ta", "ia", ("zh", "co")),
            first,
            second,
            time,
            first,
            first,
            second,
            second,
            time,
            time,
        ),
        out_specs=(first, second, time, first, first, second, second, time, time),
        check_vma=False,
    )
```

```python
import jax
import jax.numpy as jnp
from jax import lax
from jax.experimental import pallas as pl
from jax.experimental.pallas import tpu as pltpu
from jax.sharding import PartitionSpec as P

ADAM_STEP = 20


beta_one = 0.9
beta_two = 0.99
step_rate = 0.02
tiny_eps = 1e-08


def adam(value, grad, mean, square, count):
    drift = beta_one * mean + (1.0 - beta_one) * grad
    spread = beta_two * square + (1.0 - beta_two) * grad * grad
    fixed_one = 1.0 - beta_one**count
    fixed_two = 1.0 - beta_two**count
    value = value - step_rate * (drift / fixed_one) / (jnp.sqrt(spread / fixed_two) + tiny_eps)
    return (value, drift, spread)


def swap(x, axis, k):
    n = lax.axis_size(axis)
    return lax.ppermute(x, axis, [(i, i ^ k) for i in range(n)])


def pick(flag, x, y):
    return jnp.where(flag, y, x), jnp.where(flag, x, y)


def gather_ta(x):
    ta = lax.axis_index("ta")
    p = [x] + [swap(x, "ta", k) for k in (1, 2, 3)]
    odd, high = (ta & 1) == 1, (ta & 2) == 2
    q0, q1 = pick(odd, p[0], p[1])
    q2, q3 = pick(odd, p[2], p[3])
    q0, q2 = pick(high, q0, q2)
    q1, q3 = pick(high, q1, q3)
    return [q0, q1, q2, q3]


def stack_columns(x):
    return jnp.concatenate([x[:, n * 128 : (n + 1) * 128] for n in range(x.shape[1] // 128)], axis=0)


def unstack_columns(x, ranks):
    return jnp.concatenate([x[n * ranks : (n + 1) * ranks] for n in range(x.shape[0] // ranks)], axis=1)


def pack_kernel(f0, f1, f2, s0, s1, s2, out, state):
    rows = f0.shape[0]
    ranks = s0.shape[0]
    for p in range(out.shape[0]):
        for n, x in enumerate((s0, s1, s2)):
            for h in (0, 1):
                at = (2 * n + h) * ranks
                out[p, at : at + ranks, :] = x[:, h * 128 : (h + 1) * 128]
        out[p, 6 * ranks :, :] = f0[...]
    for n, x in enumerate((f0, f1, f2)):
        state[n * rows : (n + 1) * rows, :] = x[...]


def pack(copies, firsts, seconds):
    rows, rank = firsts[0].shape
    slots = (copies, rows + 6 * seconds[0].shape[0], rank)
    return pl.pallas_call(
        pack_kernel,
        out_shape=[
            jax.ShapeDtypeStruct(slots, jnp.float32),
            jax.ShapeDtypeStruct((3 * rows, rank), jnp.float32),
        ],
        in_specs=[pl.BlockSpec(memory_space=pltpu.VMEM)] * 6,
        out_specs=[pl.BlockSpec(memory_space=pltpu.VMEM)] * 2,
    )(*firsts, *seconds)


def join_cores(x):
    low, high = pick(lax.axis_index("co") == 1, x, swap(x, "co", 1))
    return jnp.stack([low, high], axis=1)


def gather_first(pair):
    rank = pair.shape[1]
    x = join_cores(pair.reshape(2, -1, rank))
    x = x.reshape((-1,) + x.shape[2:])
    return jnp.stack(gather_ta(x), axis=1).reshape(-1, rank)


def core_half(part, extra):
    one = lax.axis_index("co") == 1
    quarter = part.shape[0] // 4
    q = [part[n * quarter : (n + 1) * quarter] for n in range(4)]
    keep0, send0 = pick(one, q[0], q[1])
    keep1, send1 = pick(one, q[2], q[3])
    keep = jnp.concatenate([keep0, keep1], axis=0)
    got = swap(jnp.concatenate([send0, send1] + extra, axis=0), "co", 1)
    half = keep.shape[0]
    return keep + got[:half], [extra[0] + got[half:]] if extra else []


def bf16_pair(x):
    top = lax.reduce_precision(x, 8, 7)
    return [top.astype(jnp.bfloat16), (x - top).astype(jnp.bfloat16)]


def fold(x, rows):
    return jnp.concatenate([x[n * rows : (n + 1) * rows] for n in range(x.shape[0] // rows)], axis=1)


def time_of(got, rank):
    r = got.shape[1] // 2
    line = jnp.sum(got[:, :r].astype(jnp.float32) + got[:, r:].astype(jnp.float32), axis=0)
    return jnp.concatenate(
        [line[:, n * rank : (n + 1) * rank] for n in range(line.shape[1] // rank)], axis=0
    )


def spread_slots(stacked, extra):
    ni = lax.axis_size("ia")
    wide = stacked.astype(jnp.bfloat16)
    half = wide.shape[0] // 2
    ranks = half // 4
    flat = jnp.concatenate(
        [unstack_columns(wide[:half], ranks), unstack_columns(wide[half:], ranks)] + extra, axis=0
    )
    return jnp.broadcast_to(flat, (ni,) + flat.shape)


def spread_second(slots, ranks):
    ni, _, width = slots.shape
    got = lax.all_to_all(slots, "ia", 0, 0)
    b16 = jnp.concatenate(
        [
            got[:, :ranks].reshape(ni * ranks, width),
            got[:, ranks : 2 * ranks].reshape(ni * ranks, width),
        ],
        axis=1,
    )
    return b16, got[:, 2 * ranks :]


def sum_second(slots, ranks):
    got = lax.all_to_all(slots, "ia", 0, 0)
    total = jnp.sum(got[:, : 2 * ranks].astype(jnp.float32), axis=0)
    return jnp.concatenate([total[:ranks], total[ranks:]], axis=1), got[:, 2 * ranks :]


def step_kernel(readings, a16, b16, times, part_first, slots, part_time, total):
    block = readings.shape[0]
    now = pl.program_id(0)
    af = a16[...].astype(jnp.float32)
    bf = b16[...]

    @pl.when(now == 0)
    def _():
        total[...] = jnp.zeros_like(total)
        part_first[...] = jnp.zeros_like(part_first)
        part_time[...] = jnp.zeros_like(part_time)

    row = lax.broadcasted_iota(jnp.int32, part_time.shape, 0)
    first, time = part_first[...], part_time[...]
    all_scaled, all_slope = [], []
    for t in range(block):
        cf = times[now * block + t]
        scaled = (af * cf).astype(jnp.bfloat16)
        model = jnp.dot(scaled, bf, preferred_element_type=jnp.float32)
        inverse = 1.0 / model
        slope = inverse * (1.0 - readings[t].astype(jnp.float32) * inverse)
        slope = slope.astype(jnp.bfloat16)
        cross = lax.dot_general(
            slope, bf, (((1,), (1,)), ((), ())), preferred_element_type=jnp.float32
        )
        first = first + cross * cf
        line = jnp.sum(cross * af, axis=0, keepdims=True)
        time = time + jnp.where(row == now * block + t, line, 0.0)
        all_scaled.append(scaled)
        all_slope.append(slope)
    part_first[...] = first
    part_time[...] = time
    total[...] += lax.dot_general(
        jnp.concatenate(all_scaled, axis=0),
        jnp.concatenate(all_slope, axis=0),
        (((0,), (0,)), ((), ())),
        preferred_element_type=jnp.float32,
    )

    @pl.when(now == pl.num_programs(0) - 1)
    def _():
        count = slots.shape[0]
        ranks = total.shape[0] // count
        half = total.shape[1] // 2
        for p in range(count):
            rows = total[p * ranks : (p + 1) * ranks, :]
            flat = jnp.concatenate([rows[:, :half], rows[:, half:]], axis=0)
            slots[p] = flat.astype(slots.dtype)


def step_parts(readings, a16, b16, c16, ni):
    times, rows, cols = readings.shape
    rank = a16.shape[1]
    block = 4
    return pl.pallas_call(
        step_kernel,
        grid=(times // block,),
        in_specs=[
            pl.BlockSpec((block, rows, cols), lambda k: (k, 0, 0)),
            pl.BlockSpec((rows, rank), lambda k: (0, 0)),
            pl.BlockSpec((rank, cols), lambda k: (0, 0)),
            pl.BlockSpec((times, 1, rank), lambda k: (0, 0, 0)),
        ],
        out_specs=[
            pl.BlockSpec((rows, rank), lambda k: (0, 0)),
            pl.BlockSpec((ni, 2 * rank // ni, cols // 2), lambda k: (0, 0, 0)),
            pl.BlockSpec((16, rank), lambda k: (0, 0)),
        ],
        out_shape=[
            jax.ShapeDtypeStruct((rows, rank), jnp.float32),
            jax.ShapeDtypeStruct((ni, 2 * rank // ni, cols // 2), jnp.bfloat16),
            jax.ShapeDtypeStruct((16, rank), jnp.float32),
        ],
        scratch_shapes=[pltpu.VMEM((rank, cols), jnp.float32)],
        compiler_params=pltpu.CompilerParams(vmem_limit_bytes=50 * 2**20),
        cost_estimate=pl.CostEstimate(
            flops=6 * times * rows * cols * rank,
            bytes_accessed=2 * times * rows * cols,
            transcendentals=times * rows * cols,
        ),
    )(readings, a16, b16, c16.astype(jnp.float32)[:, None, :])


def body(
    readings,
    factor_first,
    factor_second,
    factor_time,
    mean_first,
    square_first,
    mean_second,
    square_second,
    mean_time,
    square_time,
):
    ni, nt = lax.axis_size("ia"), lax.axis_size("ta")
    nj = lax.axis_size("zh") * lax.axis_size("co")
    whole_i = readings.shape[1] * ni
    whole_j = readings.shape[2] * nj
    whole_k = readings.shape[0] * nt
    n_time, rank = factor_time.shape
    scale_first = rank / (whole_j * whole_k)
    scale_second = rank / (whole_i * whole_k)
    scale_time = rank / (whole_i * whole_j)
    rows = factor_first.shape[0]
    ranks, cols = factor_second.shape
    flat = 2 * ranks
    zh, ta = lax.axis_index("zh"), lax.axis_index("ta")
    high = zh == 1

    slots, own_first = pack(
        1,
        (factor_first, mean_first, square_first),
        (factor_second, mean_second, square_second),
    )
    got = jnp.stack(gather_ta(slots[0]), axis=0)
    wide_second, wide_mean, wide_square = [
        got[:, n * flat : (n + 1) * flat].reshape(nt * flat, rank) for n in (0, 1, 2)
    ]
    a16 = got[:, 3 * flat :].astype(jnp.bfloat16).reshape(nt * rows, rank)

    pad = [a16[n * ranks : (n + 1) * ranks] for n in range(4)]
    slots = spread_slots(wide_second, [jnp.concatenate(pad, axis=1)])
    slots, a16 = lax.optimization_barrier((slots, a16))
    b16, _ = spread_second(slots, ranks)
    a16 = join_cores(a16[None]).reshape(-1, rank)
    low, up = pick(high, a16, swap(a16, "zh", 1))
    a16 = jnp.concatenate([low, up], axis=0)
    c16 = factor_time.astype(jnp.bfloat16)
    part_first, slots, part_time = step_parts(readings, a16, b16, c16, ni)
    second, _ = sum_second(slots, ranks)
    part, [part_time] = core_half(part_first, [part_time])
    sent = jnp.concatenate([part, part_time, own_first], axis=0)
    came = swap(sent, "zh", 1)
    low, up = pick(high, own_first, came[9 * rows :])
    pair_first, pair_mean, pair_square = [
        jnp.concatenate([low[n : n + rows], up[n : n + rows]], axis=0)
        for n in (0, rows, 2 * rows)
    ]
    part = part + came[: 8 * rows]
    time_ja = part_time + came[8 * rows : 9 * rows]
    part = part.reshape(2, nt, rows, rank).transpose(1, 0, 2, 3).reshape(nt, 2 * rows, rank)
    second = stack_columns(second)
    slot = lambda t: jnp.concatenate(
        [lax.dynamic_index_in_dim(part, t, 0, keepdims=False), second], axis=0
    ).astype(jnp.bfloat16)
    got = [slot(ta)] + [swap(slot(ta ^ k), "ta", k) for k in (1, 2, 3)]
    got = [x.astype(jnp.float32) for x in got]
    got = (got[0] + got[1]) + (got[2] + got[3])
    grad_first, grad_second = got[: 2 * rows], got[2 * rows :]
    count = ADAM_STEP + 1
    wide_second, wide_mean, wide_square = adam(
        wide_second, grad_second * scale_second, wide_mean, wide_square, count
    )
    pair_first, pair_mean, pair_square = adam(
        pair_first, grad_first * scale_first, pair_mean, pair_square, count
    )

    slots = spread_slots(wide_second, bf16_pair(fold(time_ja, ranks // 2)))
    b16, came = spread_second(slots, ranks)
    a16 = gather_first(pair_first.astype(jnp.bfloat16))
    time_sum = time_of(came, rank)[:n_time]
    factor_time, mean_time, square_time = adam(
        factor_time, time_sum * scale_time, mean_time, square_time, count
    )
    c16 = factor_time.astype(jnp.bfloat16)
    part_first, slots, part_time = step_parts(readings, a16, b16, c16, ni)
    part, [part_time] = core_half(part_first, [part_time])
    line = jnp.concatenate(bf16_pair(fold(part_time, ranks // 2)), axis=0)
    line = jnp.broadcast_to(line, (ni,) + line.shape)
    second, came = sum_second(jnp.concatenate([slots, line], axis=1), ranks)
    keep, send = pick(high, part[: 4 * rows], part[4 * rows :])
    part = keep + swap(send, "zh", 1)
    time_sum = time_of(came, rank)
    time_sum = time_sum + swap(time_sum, "zh", 1)
    slots = jnp.concatenate(
        [part.reshape(nt, rows, rank), stack_columns(second).reshape(nt, flat, rank)], axis=1
    )
    slot = lambda t: lax.dynamic_index_in_dim(slots, t, 0, keepdims=False)
    got = [slot(ta)] + [swap(slot(ta ^ k), "ta", k) for k in (1, 2, 3)]
    got = (got[0] + got[1]) + (got[2] + got[3])
    count = ADAM_STEP + 2
    first = lambda x: jnp.where(high, x[rows:], x[:rows])
    own = lambda x: unstack_columns(lax.dynamic_slice_in_dim(x, ta * flat, flat, axis=0), ranks)
    factor_first, mean_first, square_first = adam(
        first(pair_first), got[:rows] * scale_first, first(pair_mean), first(pair_square), count
    )
    factor_second, mean_second, square_second = adam(
        own(wide_second),
        unstack_columns(got[rows:], ranks) * scale_second,
        own(wide_mean),
        own(wide_square),
        count,
    )
    factor_time, mean_time, square_time = adam(
        factor_time, time_sum[:n_time] * scale_time, mean_time, square_time, count
    )
    return (
        factor_first,
        factor_second,
        factor_time,
        mean_first,
        square_first,
        mean_second,
        square_second,
        mean_time,
        square_time,
    )


def solution(mesh):
    shape = (mesh.shape["ia"], 2, mesh.shape["ja"] // 2, mesh.shape["ta"])
    mesh = jax.sharding.Mesh(mesh.devices.reshape(shape), ("ia", "zh", "co", "ta"))
    first = P(("ia", "zh", "co", "ta"), None)
    second = P("ia", ("zh", "co", "ta"))
    time = P("ta", None)
    return jax.shard_map(
        body,
        mesh=mesh,
        in_specs=(
            P("ta", "ia", ("zh", "co")),
            first,
            second,
            time,
            first,
            first,
            second,
            second,
            time,
            time,
        ),
        out_specs=(first, second, time, first, first, second, second, time, time),
        check_vma=False,
    )
```
